128 devices in a mesh: ctx: 64 (over y, z, x_lo, core), fsdp: 2 (over x_hi).
Axes of the slice: x: 4 (x_hi: 2, x_lo: 2; x = x_hi * 2 + x_lo), y: 4, z: 4, core: 2. Of those that a mesh axis runs over, the one named last changes fastest.
Arguments:
- hidden_in: bfloat16 [2, 8192, 1024], P('fsdp', 'ctx'), may hold values from -6 to 6
- doc_ids: int32 [2, 8192], P('fsdp'), may hold values from 0 to 2, as said below
- block_map: int32 [64], replicated, may hold values from 0 to 63, each once
- attn_gain: bfloat16 [1024], P('fsdp'), may hold values from 0.5 to 1.5
- attn_shift: bfloat16 [1024], P('fsdp'), may hold values from -1.5 to 1.5
- mlp_gain: bfloat16 [1024], P('fsdp'), may hold values from 0.5 to 1.5
- mlp_shift: bfloat16 [1024], P('fsdp'), may hold values from -1.5 to 1.5
- qkv_weight: bfloat16 [1024, 3072], P('fsdp'), may hold values from -0.1875 to 0.1875
- qkv_bias: bfloat16 [3072], P('fsdp'), may hold values from -1.5 to 1.5
- out_weight: bfloat16 [1024, 1024], P('fsdp'), may hold values from -1.5 to 1.5
- out_bias: bfloat16 [1024], P('fsdp'), may hold values from -1.5 to 1.5
- in_weight: bfloat16 [1024, 4096], P('fsdp'), may hold values from -0.1875 to 0.1875
- in_bias: bfloat16 [4096], P('fsdp'), may hold values from -1.5 to 1.5
- proj_weight: bfloat16 [4096, 1024], P('fsdp'), may hold values from -0.09375 to 0.09375
- proj_bias: bfloat16 [1024], P('fsdp'), may hold values from -1.5 to 1.5
- cotangent: bfloat16 [2, 8192, 1024], P('fsdp', 'ctx'), may hold values from -6 to 6
Outputs:
- hidden_out: bfloat16 [2, 8192, 1024], P('fsdp', 'ctx')
- hidden_grad: float32 [2, 8192, 1024], P('fsdp', 'ctx')
- attn_gain_grad: float32 [1024], P('fsdp')
- attn_shift_grad: float32 [1024], P('fsdp')
- mlp_gain_grad: float32 [1024], P('fsdp')
- mlp_shift_grad: float32 [1024], P('fsdp')
- qkv_weight_grad: float32 [1024, 3072], P('fsdp')
- qkv_bias_grad: float32 [3072], P('fsdp')
- out_weight_grad: float32 [1024, 1024], P('fsdp')
- out_bias_grad: float32 [1024], P('fsdp')
- in_weight_grad: float32 [1024, 4096], P('fsdp')
- in_bias_grad: float32 [4096], P('fsdp')
- proj_weight_grad: float32 [4096, 1024], P('fsdp')
- proj_bias_grad: float32 [1024], P('fsdp')
The draws below stay inside these ranges and needn't reach their ends.
Inputs may be any that keep to these rules, and one draw needn't show every extreme that they name: `doc_ids`: each row is nondecreasing along the stream, holds every document number, and document 0 covers at least the first half of the stream. `block_map`: a permutation of the block pairs.
All inputs are finite; a program needn't handle non-finite values.
Results may differ from the reference program's by a relative error of at most 0.012.
Values may be sent and summed in bfloat16 or wider, within the bound.
No kernel may reach another device: no remote copies, remote signals or barrier semaphores. Data moves between devices by JAX's collectives and lax.ppermute only.
A program may use at most 320 MiB of HBM per device.

```python
import jax
import jax.numpy as jnp
from jax import lax

D = 1024
HEADS = 16
HEAD_DIM = 64
ROT = 16
FF = 4096
DOCS = 3
TOK_DEV = 128
PAIRS = 64
SPLITS = 2
STREAM = 8192


def draw_doc_ids(key, part):
    key = jax.random.fold_in(key, 7)
    first_key, second_key = jax.random.split(key)
    first_length = jax.random.randint(first_key, (SPLITS,), STREAM // 2, STREAM // 2 + STREAM // 8 + 1)
    remain = STREAM - first_length
    cut_at = first_length + remain // 3 + jax.random.randint(second_key, (SPLITS,), 0, remain // 3 + 1)
    places = jnp.arange(STREAM, dtype=jnp.int32)[None, :]
    later = (places >= first_length[:, None]).astype(jnp.int32)
    latest = (places >= cut_at[:, None]).astype(jnp.int32)
    return (later + latest).astype(jnp.int32)


def shard_levels(own_key, dims, cuts, least, largest):
    def one(dim, blocks):
        draws = jax.random.uniform(jax.random.fold_in(jax.random.fold_in(own_key, 6), dim), (blocks,), jnp.float32, least / len(cuts), largest / len(cuts))
        return jnp.repeat(jnp.exp(draws), dims[dim] // blocks).reshape((-1,) + (1,) * (len(dims) - dim - 1))

    loudness = one(*cuts[0])
    for cut in cuts[1:]:
        loudness = loudness * one(*cut)
    return loudness


def gaussian(key, extent, scale, limit, cuts=(), held_as=jnp.bfloat16):
    factor_of = shard_levels(key, extent, cuts, -0.22, 0.18) if cuts else 1.0
    drawn = jax.random.normal(key, extent, jnp.float32) * scale * factor_of
    return jnp.minimum(jnp.maximum(drawn, -limit), limit).astype(held_as)


def setup_inputs(seed: int = 0) -> dict:
    streams_of = jax.random.split(jax.random.key(seed), 17)
    return {
        "hidden_in": gaussian(streams_of[0], (SPLITS, STREAM, D), 1.0, 6.0, ((0, 2), (1, 64))),
        "doc_ids": draw_doc_ids(jax.random.fold_in(streams_of[16], 71), 0),
        "block_map": jax.random.permutation(streams_of[2], PAIRS).astype(jnp.int32),
        "attn_gain": jnp.clip(1.0 + 0.1 * jax.random.normal(streams_of[3], (D,), jnp.float32), 0.5, 1.5).astype(jnp.bfloat16),
        "attn_shift": gaussian(streams_of[4], (D,), 0.3, 1.5, ((0, 2),)),
        "mlp_gain": jnp.clip(1.0 + 0.1 * jax.random.normal(streams_of[5], (D,), jnp.float32), 0.5, 1.5).astype(jnp.bfloat16),
        "mlp_shift": gaussian(streams_of[6], (D,), 0.3, 1.5, ((0, 2),)),
        "qkv_weight": gaussian(streams_of[7], (D, 3 * D), D ** -0.5, 0.1875, ((0, 2),)),
        "qkv_bias": gaussian(streams_of[8], (3 * D,), 0.3, 1.5, ((0, 2),)),
        "out_weight": gaussian(streams_of[9], (D, D), (D // 64) ** -0.5, 1.5, ((0, 2),)),
        "out_bias": gaussian(streams_of[10], (D,), 0.3, 1.5, ((0, 2),)),
        "in_weight": gaussian(streams_of[11], (D, FF), D ** -0.5, 0.1875, ((0, 2),)),
        "in_bias": gaussian(streams_of[12], (FF,), 0.3, 1.5, ((0, 2),)),
        "proj_weight": gaussian(streams_of[13], (FF, D), FF ** -0.5, 0.09375, ((0, 2),)),
        "proj_bias": gaussian(streams_of[14], (D,), 0.3, 1.5, ((0, 2),)),
        "cotangent": gaussian(streams_of[15], (SPLITS, STREAM, D), 1.0, 6.0, ((0, 2), (1, 64))),
    }


EPS = 1e-05
NEG_FILL = -1e+30
HIGHEST_PREC = lax.Precision.HIGHEST

@jax.custom_vjp
def low(v):
    return lax.optimization_barrier(v.astype(jnp.bfloat16)).astype(jnp.float32)

@jax.custom_vjp
def low_back(v):
    return v

def low_keep(v):
    return (low(v), None)

def low_pass(kept, grad):
    return (grad,)

def back_keep(v):
    return (v, None)

def back_low(kept, grad):
    return (low(grad),)
low.defvjp(low_keep, low_pass)
low_back.defvjp(back_keep, back_low)

def norm_apply(hidden, gain, shift):
    centre = lax.optimization_barrier(jnp.mean(hidden, axis=-1, keepdims=True))
    moved = hidden - centre
    spread = lax.optimization_barrier(jnp.mean(moved * moved, axis=-1, keepdims=True))
    return moved * lax.rsqrt(spread + EPS) * gain + shift

def frequencies():
    return 10000.0 ** (-(jnp.arange(0, ROT, 2).astype(jnp.float32) / ROT))

def rotate(heads_in, angles):
    cosine = jnp.cos(angles)
    sine = jnp.sin(angles)
    cosine = jnp.concatenate([cosine, cosine], axis=-1)[..., None, :]
    sine = jnp.concatenate([sine, sine], axis=-1)[..., None, :]
    turned_part = heads_in[..., :ROT]
    first_half = turned_part[..., :ROT // 2]
    second_half = turned_part[..., ROT // 2:]
    turned = turned_part * cosine + jnp.concatenate([-second_half, first_half], axis=-1) * sine
    return jnp.concatenate([turned, heads_in[..., ROT:]], axis=-1)

def stream_positions(block_map, half_rows):
    pair_count = block_map.shape[0]
    offsets = jnp.arange(half_rows, dtype=jnp.int32)
    lower_rows = block_map[:, None] * half_rows + offsets[None, :]
    upper_rows = (2 * pair_count - 1 - block_map)[:, None] * half_rows + offsets[None, :]
    return jnp.concatenate([lower_rows, upper_rows], axis=1).astype(jnp.int32)

def attention(queries, keys, values, doc_ids):
    block_rows = min(512, STREAM)
    block_count = STREAM // block_rows
    scale = HEAD_DIM ** (-0.5)
    where_at = jnp.arange(STREAM, dtype=jnp.int32)

    def one_block(block_index):
        group_id = block_index // block_count
        row_start = block_index % block_count * block_rows
        query_block = lax.dynamic_slice_in_dim(lax.dynamic_index_in_dim(queries, group_id, 0, False), row_start, block_rows, 0)
        key_group = lax.dynamic_index_in_dim(keys, group_id, 0, False)
        value_group = lax.dynamic_index_in_dim(values, group_id, 0, False)
        segment = lax.dynamic_index_in_dim(doc_ids, group_id, 0, False)
        query_doc = lax.dynamic_slice_in_dim(segment, row_start, block_rows, 0)
        query_pos = row_start + jnp.arange(block_rows, dtype=jnp.int32)
        raw_scores = jnp.einsum('qhd,khd->hqk', query_block, key_group, precision=HIGHEST_PREC)
        scores = low_back(scale * raw_scores)
        allowed = (where_at[None, :] <= query_pos[:, None]) & (segment[None, :] == query_doc[:, None])
        scores = jnp.where(allowed[None], scores, NEG_FILL)
        row_top = lax.optimization_barrier(jnp.max(scores, axis=-1, keepdims=True))
        weights = jnp.exp(scores - row_top)
        chances = weights / lax.optimization_barrier(jnp.sum(weights, axis=-1, keepdims=True))
        return jnp.einsum('hqk,khd->qhd', low(chances), value_group, precision=HIGHEST_PREC)
    blocks = lax.map(jax.checkpoint(one_block), jnp.arange(SPLITS * block_count, dtype=jnp.int32))
    return blocks.reshape(SPLITS, STREAM, HEADS * HEAD_DIM)

def reference(hidden_in, doc_ids, block_map, attn_gain, attn_shift, mlp_gain, mlp_shift, qkv_weight, qkv_bias, out_weight, out_bias, in_weight, in_bias, proj_weight, proj_bias, cotangent):
    layout = stream_positions(block_map, TOK_DEV // 2).reshape(-1)
    inverse = jnp.argsort(layout).astype(jnp.int32)
    hidden = hidden_in.astype(jnp.float32)[:, inverse]
    upstream = cotangent.astype(jnp.float32)[:, inverse]
    labels = jnp.arange(DOCS, dtype=jnp.int32)
    starts = lax.optimization_barrier(jnp.sum((doc_ids[:, None, :] < labels[None, :, None]).astype(jnp.int32), axis=2))
    doc_first = lax.optimization_barrier(jnp.sum(jnp.where(doc_ids[:, :, None] == labels[None, None, :], starts[:, None, :], 0), axis=2))
    relative = (jnp.arange(STREAM, dtype=jnp.int32)[None, :] - doc_first).astype(jnp.float32)
    angles = relative[:, :, None] * frequencies()[None, None, :]

    def forward(hidden, attn_gain, attn_shift, mlp_gain, mlp_shift, qkv_weight, qkv_bias, out_weight, out_bias, in_weight, in_bias, proj_weight, proj_bias):
        normed = low(norm_apply(hidden, attn_gain, attn_shift))
        project = low_back(jnp.einsum('sti,io->sto', normed, qkv_weight, precision=HIGHEST_PREC) + qkv_bias)
        shaped = project.reshape(SPLITS, STREAM, 3, HEADS, HEAD_DIM)
        queries = low(rotate(shaped[:, :, 0], angles))
        keys = low(rotate(shaped[:, :, 1], angles))
        values = low(shaped[:, :, 2])
        mixed_sum = attention(queries, keys, values, doc_ids)
        mixed_sum = low(low_back(mixed_sum))
        branch_attn = jnp.einsum('sti,io->sto', mixed_sum, out_weight, precision=HIGHEST_PREC) + out_bias
        normed_mlp = low(norm_apply(hidden, mlp_gain, mlp_shift))
        inner_act = low_back(jnp.einsum('sti,io->sto', normed_mlp, in_weight, precision=HIGHEST_PREC) + in_bias)
        active = low(jax.nn.gelu(inner_act, approximate=False))
        branch_mlp = jnp.einsum('sti,io->sto', active, proj_weight, precision=HIGHEST_PREC) + proj_bias
        return hidden + branch_attn + branch_mlp
    result, pullback = jax.vjp(forward, hidden, attn_gain.astype(jnp.float32), attn_shift.astype(jnp.float32), mlp_gain.astype(jnp.float32), mlp_shift.astype(jnp.float32), qkv_weight.astype(jnp.float32), qkv_bias.astype(jnp.float32), out_weight.astype(jnp.float32), out_bias.astype(jnp.float32), in_weight.astype(jnp.float32), in_bias.astype(jnp.float32), proj_weight.astype(jnp.float32), proj_bias.astype(jnp.float32))
    gradients = pullback(upstream)
    hidden_out = result[:, layout].astype(jnp.bfloat16)
    hidden_grad = gradients[0][:, layout]
    return (hidden_out, hidden_grad, gradients[1], gradients[2], gradients[3], gradients[4], gradients[5], gradients[6], gradients[7], gradients[8], gradients[9], gradients[10], gradients[11], gradients[12])
```

```python
import functools
import math

import jax
import jax.numpy as jnp
from jax import lax
from jax.experimental import pallas as pl
from jax.experimental.pallas import tpu as pltpu
from jax.sharding import Mesh
from jax.sharding import PartitionSpec as P

ROT = 16
EPS = 1e-05
NEG_FILL = -1e30
BF = jnp.bfloat16
F32 = jnp.float32
RING = ("xh", "xl")
PLANE = ("y", "z")
MIB = 1 << 20

NN = (((1,), (0,)), ((), ()))
NT = (((1,), (1,)), ((), ()))
TN = (((0,), (0,)), ((), ()))


def mm(left, right, dims=NN):
    return lax.dot_general(left, right, dims, preferred_element_type=F32)


def mult(value, step):
    return pl.multiple_of(value, step)


def whole(space=pltpu.VMEM):
    return pl.BlockSpec(memory_space=space)


def call(body, outs, ins, scratch=(), flops=0, moved=0, limit=48):
    return pl.pallas_call(
        body,
        out_shape=outs,
        in_specs=ins,
        out_specs=[whole() for _ in outs],
        scratch_shapes=list(scratch),
        cost_estimate=pl.CostEstimate(flops=flops, bytes_accessed=moved, transcendentals=0),
        compiler_params=pltpu.CompilerParams(vmem_limit_bytes=limit * MIB),
    )


def to_all(array_in, axes, count):
    copies = jnp.broadcast_to(array_in[None], (count,) + array_in.shape)
    return lax.all_to_all(copies, axes, 0, 0, tiled=True)


def swap(array_in, axis):
    return lax.ppermute(array_in, axis, [(0, 1), (1, 0)])


def in_order(first, mine, other):
    return jnp.where(first, jnp.stack([mine, other]), jnp.stack([other, mine]))


def turn(tile, cosine, sine_low, sine_high):
    return (
        tile * cosine
        + pltpu.roll(tile, 120, 1) * sine_low
        + pltpu.roll(tile, 8, 1) * sine_high
    )


def sine_parts(sine, sign):
    spot = lax.broadcasted_iota(jnp.int32, sine.shape, 1) % 64
    low = jnp.where(spot < 8, -sign * sine, 0.0)
    high = jnp.where((spot >= 8) & (spot < 16), sign * sine, 0.0)
    return low, high


def project_kernel(hidden, gain, shift, weight, bias, cosine, sine, send, normed):
    for block in range(4):
        stream, half_x = block // 2, block % 2
        rows = pl.ds(block * 128, 128)
        moved = hidden[rows, :].astype(F32)
        moved = moved - jnp.mean(moved, axis=1, keepdims=True)
        spread = jnp.mean(moved * moved, axis=1, keepdims=True)
        norm = (moved * lax.rsqrt(spread + EPS) * gain[...] + shift[...]).astype(BF)
        normed[rows, :] = norm
        project = mm(norm, weight[...]) + bias[...]
        cos = cosine[rows, :]
        low, high = sine_parts(sine[rows, :], 1.0)
        left = lax.broadcasted_iota(jnp.int32, (64, 128), 1) < 64
        left_all = lax.broadcasted_iota(jnp.int32, (128, 128), 1) < 64
        for pair in range(2):
            at = pair * 128
            query = turn(project[:, at : at + 128], cos, low, high) * 0.125
            key = turn(project[:, 256 + at : 384 + at], cos, low, high)
            value = project[:, 512 + at : 640 + at]
            q_low, q_high = query[:64], query[64:]
            packed = (
                jnp.where(left, q_low, pltpu.roll(q_high, 64, 1)).astype(BF),
                jnp.where(left, pltpu.roll(q_low, 64, 1), q_high).astype(BF),
            )
            key_value = (
                jnp.where(left_all, key, pltpu.roll(value, 64, 1)).astype(BF),
                jnp.where(left_all, pltpu.roll(key, 64, 1), value).astype(BF),
            )
            for member in range(2):
                head = pair * 2 + member
                for half in range(2):
                    target = stream * 8 + head * 2 + half
                    send[target, pl.ds(half_x * 128, 128), :] = key_value[member]
                    for core in range(2):
                        quarter = half * 2 + core
                        send[target, pl.ds(256 + core * 32 + half_x * 16, 16), :] = packed[member][
                            quarter * 16 : quarter * 16 + 16
                        ]


def mixed_grad_kernel(upstream, weight, send):
    left = lax.broadcasted_iota(jnp.int32, (64, 128), 1) < 64
    for block in range(4):
        stream, half_x = block // 2, block % 2
        grads = mm(upstream[pl.ds(block * 128, 128), :], weight[...], NT)
        for pair in range(2):
            tile = grads[:, pair * 128 : pair * 128 + 128]
            low, high = tile[:64], tile[64:]
            packed = (
                jnp.where(left, low, pltpu.roll(high, 64, 1)).astype(BF),
                jnp.where(left, pltpu.roll(low, 64, 1), high).astype(BF),
            )
            for member in range(2):
                for half in range(2):
                    target = stream * 8 + (pair * 2 + member) * 2 + half
                    for core in range(2):
                        quarter = half * 2 + core
                        send[target, pl.ds(core * 32 + half_x * 16, 16), :] = packed[member][
                            quarter * 16 : quarter * 16 + 16
                        ]


KEY_TILE = 512


def attend_kernel(
    place, block_map, own, other, grad_own, grad_other, out_own, out_other,
    kv, kv_turned, q_grad, scores, chances, key_sums, rows_out,
):
    core, quarter, second, third = place[0], place[1], place[2], place[3]
    left16 = lax.broadcasted_iota(jnp.int32, (16, 128), 1) < 64
    left = lax.broadcasted_iota(jnp.int32, (128, 128), 1) < 64

    def fill(source, grad_source, from_core):
        @pl.loop(0, 32)
        def _(i):
            group, half_x = i // 2, i % 2
            block = block_map[i * 2 + from_core]
            mirror = 127 - block
            kv[pl.ds(mult(block * 64, 64), 64), :] = source[group, pl.ds(mult(half_x * 128, 64), 64), :]
            kv[pl.ds(mult(mirror * 64, 64), 64), :] = source[
                group, pl.ds(mult(half_x * 128 + 64, 64), 64), :
            ]
            spot = core * 32 + half_x * 16
            query = source[group, pl.ds(mult(256 + spot, 16), 16), :].astype(F32)
            grad = grad_source[group, pl.ds(mult(spot, 16), 16), :].astype(F32)
            q_grad[pl.ds(mult(block * 16, 16), 16), :] = jnp.where(
                left16, query, pltpu.roll(grad, 64, 1)
            ).astype(BF)
            q_grad[pl.ds(mult(mirror * 16, 16), 16), :] = jnp.where(
                left16, pltpu.roll(query, 64, 1), grad
            ).astype(BF)

    fill(own, grad_own, core)
    fill(other, grad_other, 1 - core)

    @pl.loop(0, 64)
    def _(c):
        cut = pl.ds(mult(c * 128, 128), 128)
        kv_turned[:, cut] = kv[cut, :].astype(F32).T.astype(BF)
        key_sums[:, cut] = jnp.zeros((128, 128), F32)

    row = lax.broadcasted_iota(jnp.int32, (128, 1), 0)
    offset = (row // 16) * 64 + quarter * 16 + row % 16
    spots = lax.broadcasted_iota(jnp.int32, (128, KEY_TILE), 1)

    def start_of(position):
        return jnp.where(position >= third, third, jnp.where(position >= second, second, 0))

    @pl.loop(0, 16)
    def _(step):
        tile = 15 - step
        rows = pl.ds(mult(tile * 128, 128), 128)
        base = tile * KEY_TILE
        both = q_grad[rows, :]
        query, grad = both[:, :64], both[:, 64:]
        position = base + offset
        first = start_of(position)
        low = start_of(base + quarter * 16) // KEY_TILE
        high = (start_of(base + 448 + quarter * 16 + 15) + KEY_TILE - 1) // KEY_TILE
        high = jnp.minimum(jnp.maximum(high, low), tile)

        def cut_of(j):
            return pl.ds(mult(j * KEY_TILE, KEY_TILE), KEY_TILE)

        def fold(top, part):
            for c in range(KEY_TILE // 128):
                top = jnp.maximum(top, part[:, c * 128 : c * 128 + 128])
            return top

        def plain(j, top):
            part = mm(query, kv_turned[0:64, cut_of(j)])
            scores[:, cut_of(j)] = part
            return fold(top, part)

        def masked(j, top):
            part = mm(query, kv_turned[0:64, cut_of(j)])
            key_at = spots + j * KEY_TILE
            part = jnp.where((key_at <= position) & (key_at >= first), part, NEG_FILL)
            scores[:, cut_of(j)] = part
            return fold(top, part)

        top = jnp.full((128, 128), NEG_FILL, F32)
        top = lax.fori_loop(low, high, masked, top)
        top = lax.fori_loop(high, tile, plain, top)
        top = masked(tile, top)
        row_top = jnp.max(top, axis=1, keepdims=True)

        def weigh(j, state):
            total, mixed = state
            part = jnp.exp(scores[:, cut_of(j)] - row_top)
            for c in range(KEY_TILE // 128):
                total = total + part[:, c * 128 : c * 128 + 128]
            rounded = part.astype(BF)
            chances[:, cut_of(j)] = rounded
            return total, mixed + mm(rounded, kv[cut_of(j), :])

        zero = jnp.zeros((128, 128), F32)
        total, mixed = lax.fori_loop(low, tile + 1, weigh, (zero, zero))
        share = 1.0 / jnp.sum(total, axis=1, keepdims=True)
        mixed = mixed * share
        scaled = jnp.where(left, both.astype(F32), both.astype(F32) * share)
        delta = jnp.sum(jnp.where(left, 0.0, scaled * mixed), axis=1, keepdims=True)
        grad_scaled = scaled[:, 64:].astype(BF)
        turned = scaled.T.astype(BF)
        query_turned, grad_turned = turned[:64], turned[64:]

        def back(j, query_sum):
            cut = cut_of(j)
            part = chances[:, cut]
            along = mm(grad_scaled, kv_turned[64:128, cut])
            score_grad = (part.astype(F32) * (along - delta)).astype(BF)
            key_sums[0:64, cut] += mm(query_turned, score_grad)
            key_sums[64:128, cut] += mm(grad_turned, part)
            return query_sum + mm(score_grad, kv[cut, :])

        query_sum = lax.fori_loop(low, tile + 1, back, zero)
        rows_out[rows, :] = jnp.where(left, query_sum * 0.125, mixed).astype(BF)

    @pl.loop(0, 64)
    def _(c):
        cut = pl.ds(mult(c * 128, 128), 128)
        kv[cut, :] = key_sums[:, cut].T.astype(BF)

    def spill(target, to_core):
        @pl.loop(0, 32)
        def _(i):
            group, half_x = i // 2, i % 2
            block = block_map[i * 2 + to_core]
            mirror = 127 - block
            target[group, pl.ds(mult(half_x * 128, 64), 64), :] = kv[pl.ds(mult(block * 64, 64), 64), :]
            target[group, pl.ds(mult(half_x * 128 + 64, 64), 64), :] = kv[
                pl.ds(mult(mirror * 64, 64), 64), :
            ]
            spot = 256 + half_x * 32
            target[group, pl.ds(mult(spot, 16), 16), :] = rows_out[pl.ds(mult(block * 16, 16), 16), :]
            target[group, pl.ds(mult(spot + 16, 16), 16), :] = rows_out[
                pl.ds(mult(mirror * 16, 16), 16), :
            ]

    spill(out_own, core)
    spill(out_other, 1 - core)


def collect_kernel(place, back, cosine, sine, project_grad, mixed_out, heads):
    core = place[0]
    left = lax.broadcasted_iota(jnp.int32, (128, 128), 1) < 64
    for block in range(4):
        stream, half_x = block // 2, block % 2
        rows = pl.ds(block * 128, 128)
        cos = cosine[rows, :]
        low, high = sine_parts(sine[rows, :], -1.0)
        for pair in range(2):
            pieces = []
            for member in range(2):
                base = stream * 8 + (pair * 2 + member) * 2
                cut = pl.ds(half_x * 128, 128)
                key_value = back[base, cut, :].astype(F32) + back[base + 1, cut, :].astype(F32)
                for upper in range(2):
                    for half in range(2):
                        for of_core in range(2):
                            flipped = of_core ^ core
                            spot = 256 + flipped * 64 + (half_x * 2 + upper) * 16
                            heads[
                                member, pl.ds(upper * 64 + (half * 2 + of_core) * 16, 16), :
                            ] = back[base + half, pl.ds(mult(spot, 16), 16), :]
                pieces.append((heads[member].astype(F32), key_value))
            (row0, kv0), (row1, kv1) = pieces
            at = pair * 128
            query = jnp.where(left, row0, pltpu.roll(row1, 64, 1))
            key = jnp.where(left, kv0, pltpu.roll(kv1, 64, 1))
            value = jnp.where(left, pltpu.roll(kv0, 64, 1), kv1)
            mixed = jnp.where(left, pltpu.roll(row0, 64, 1), row1)
            project_grad[rows, at : at + 128] = turn(query, cos, low, high).astype(BF)
            project_grad[rows, 256 + at : 384 + at] = turn(key, cos, low, high).astype(BF)
            project_grad[rows, 512 + at : 640 + at] = value.astype(BF)
            mixed_out[rows, at : at + 128] = mixed.astype(BF)


def feed_weights_kernel(place, normed, inner_grad, active, upstream, out_own, out_other):
    for flip, target in ((0, out_own), (1, out_other)):
        core = place[0] ^ flip
        for part in range(2):
            rows = normed[:, pl.ds(mult(part * 512 + core * 256, 256), 256)]
            for quad in range(4):
                grads = mm(rows, inner_grad[:, quad * 256 : quad * 256 + 256], TN).astype(BF)
                for n in range(2):
                    slot = part * 8 + quad * 2 + n
                    target[:, slot * 16 : slot * 16 + 16, :] = grads[:, n * 128 : n * 128 + 128].reshape(
                        16, 16, 128
                    )
        rows = active[:, pl.ds(mult(core * 512, 512), 512)]
        for quad in range(4):
            grads = mm(rows, upstream[:, quad * 256 : quad * 256 + 256], TN).astype(BF)
            for n in range(2):
                at = 256 + (quad * 2 + n) * 32
                target[:, at : at + 32, :] = grads[:, n * 128 : n * 128 + 128].reshape(16, 32, 128)


def attend_weights_kernel(place, normed, project_grad, mixed, upstream, out_own, out_other):
    for flip, target in ((0, out_own), (1, out_other)):
        core = place[0] ^ flip
        for part in range(2):
            rows = normed[:, pl.ds(mult(part * 512 + core * 256, 256), 256)]
            for block in range(3):
                grads = mm(rows, project_grad[:, block * 256 : block * 256 + 256], TN).astype(BF)
                for n in range(2):
                    slot = part * 6 + block * 2 + n
                    target[:, slot * 16 : slot * 16 + 16, :] = grads[:, n * 128 : n * 128 + 128].reshape(
                        16, 16, 128
                    )
        for block in range(2):
            columns = upstream[:, pl.ds(mult(core * 512 + block * 256, 256), 256)]
            grads = mm(mixed[...], columns, TN).astype(BF)
            for n in range(2):
                at = 192 + (block * 2 + n) * 16
                target[:, at : at + 16, :] = grads[:, n * 128 : n * 128 + 128].reshape(16, 16, 128)


def spread_kernel(place, mine, other, out, *, columns):
    here = pl.program_id(0) == 0

    def put(source):
        for at, chip, slot, count in columns:
            out[:, at : at + 128] = source[0, chip, slot : slot + count, :].astype(F32)

    @pl.when(here)
    def _():
        put(mine)

    @pl.when(jnp.logical_not(here))
    def _():
        put(other)


def spread(place, mine, other, rows, width, columns):
    shape = (1,) + mine.shape[1:]
    return pl.pallas_call(
        functools.partial(spread_kernel, columns=columns),
        out_shape=jax.ShapeDtypeStruct((32 * rows, width), F32),
        grid_spec=pltpu.PrefetchScalarGridSpec(
            num_scalar_prefetch=1,
            grid=(2, 16),
            in_specs=[
                pl.BlockSpec(shape, lambda a, g, place: (jnp.where(a == 0, g, 15), 0, 0, 0)),
                pl.BlockSpec(shape, lambda a, g, place: (jnp.where(a == 0, 0, g), 0, 0, 0)),
            ],
            out_specs=pl.BlockSpec(
                (rows, width), lambda a, g, place: ((place[0] ^ a) * 16 + g, 0)
            ),
        ),
        cost_estimate=pl.CostEstimate(
            flops=0, bytes_accessed=32 * rows * width * 6, transcendentals=0
        ),
        compiler_params=pltpu.CompilerParams(vmem_limit_bytes=32 * MIB),
    )(place, mine, other)


def shape(*sizes, dtype=BF):
    return jax.ShapeDtypeStruct(sizes, dtype)


def normalized(hidden):
    moved = hidden - jnp.mean(hidden, axis=-1, keepdims=True)
    spread_out = jnp.mean(moved * moved, axis=-1, keepdims=True)
    scale = lax.rsqrt(spread_out + EPS)
    return moved * scale, scale


def per_device(
    hidden_in, doc_ids, block_map, attn_gain, attn_shift, mlp_gain, mlp_shift, qkv_weight, qkv_bias,
    out_weight, out_bias, in_weight, in_bias, proj_weight, proj_bias, cotangent,
):
    y, z = lax.axis_index("y"), lax.axis_index("z")
    xh, xl = lax.axis_index("xh"), lax.axis_index("xl")
    core = lax.axis_index("core")
    group = y * 4 + z
    chip = xh * 2 + xl
    low_half = xh == 0
    smem = whole(pltpu.SMEM)

    hidden = to_all(hidden_in[0], RING, 4).reshape(512, 1024)

    segment = doc_ids[0]
    bounds = jnp.stack([jnp.sum((segment < label).astype(jnp.int32)) for label in (1, 2)])
    bound_parts = jnp.stack([bounds // 128, bounds % 128]).reshape(4).astype(BF)
    vectors = jnp.concatenate(
        [attn_gain, attn_shift, mlp_gain, mlp_shift, qkv_bias, in_bias, out_bias, proj_bias,
         bound_parts, jnp.zeros((508,), BF)]
    ).reshape(56, 128)
    vectors_other = swap(vectors, "xh")

    chunk = (core * 16 + group) * 16
    partner = (1 - xh) * 2 + xl

    def weight_columns(which, first_row, rows):
        return jnp.concatenate(
            [lax.dynamic_slice(qkv_weight, (first_row, k * 1024 + which * 256), (rows, 256)) for k in range(3)]
            + [lax.dynamic_slice(in_weight, (first_row, which * 1024), (rows, 1024))],
            axis=1,
        )

    piece = swap(weight_columns(partner, chunk, 16), "xh")
    piece = to_all(piece, PLANE, 16).reshape(256, 1792)
    others = in_order(core == 0, piece, swap(piece, "core")).reshape(512, 1792)
    weights = in_order(low_half, weight_columns(chip, 0, 512), others).reshape(1024, 1792)
    qkv_here, in_here = weights[:, :768], weights[:, 768:]

    pairs = in_order(low_half, vectors.reshape(-1), vectors_other.reshape(-1))
    a_gain = pairs[:, 0:512].reshape(1, 1024).astype(F32)
    a_shift = pairs[:, 512:1024].reshape(1, 1024).astype(F32)
    m_gain = pairs[:, 1024:1536].reshape(1, 1024).astype(F32)
    m_shift = pairs[:, 1536:2048].reshape(1, 1024).astype(F32)
    qkv_bias_all = pairs[:, 2048:3584].reshape(3, 1024).astype(F32)
    qkv_bias_here = lax.dynamic_slice(qkv_bias_all, (0, chip * 256), (3, 256)).reshape(1, 768)
    in_bias_here = lax.dynamic_slice(
        pairs[:, 3584:5632].reshape(1, 4096), (0, chip * 1024), (1, 1024)
    ).astype(F32)
    branch_bias = (
        pairs[:, 5632:6144].reshape(1, 1024).astype(F32) + pairs[:, 6144:6656].reshape(1, 1024).astype(F32)
    )
    bound_pairs = pairs[:, 6656:6660].astype(F32).astype(jnp.int32)
    doc_bounds = bound_pairs[:, 0:2] * 128 + bound_pairs[:, 2:4]

    places = (group * 2 + jnp.arange(2, dtype=jnp.int32)) * 2 + core
    blocks = jnp.take(block_map, places)
    steps = jnp.arange(64, dtype=jnp.int32)
    position = jnp.stack(
        [blocks[:, None] * 64 + steps[None], (127 - blocks)[:, None] * 64 + steps[None]], axis=1
    ).reshape(1, 256)
    second, third = doc_bounds[:, 0:1], doc_bounds[:, 1:2]
    first = jnp.where(position >= third, third, jnp.where(position >= second, second, 0))
    relative = (position - first).astype(F32).reshape(512, 1)
    frequency = 10000.0 ** (-(jnp.arange(0, ROT, 2).astype(F32) / ROT))
    lanes = jnp.concatenate([frequency, frequency, jnp.zeros((48,), F32)])
    angles = relative * jnp.concatenate([lanes, lanes])[None]
    cosine, sine = jnp.cos(angles), jnp.sin(angles)

    cotangent, hidden = lax.optimization_barrier((cotangent, hidden))
    upstream = to_all(cotangent[0], RING, 4).reshape(512, 1024)

    send, normed = call(
        project_kernel,
        [shape(16, 320, 128), shape(512, 1024)],
        [whole()] * 7,
        flops=2 * 512 * 1024 * 768,
        moved=6 * MIB,
    )(hidden, a_gain, a_shift, qkv_here, qkv_bias_here, cosine, sine)
    heads_own = lax.all_to_all(send, PLANE, 0, 0, tiled=True)
    heads_other = swap(heads_own, "core")

    out_here = lax.dynamic_slice(out_weight, (xl * 256, 0), (256, 1024))
    (grad_send,) = call(
        mixed_grad_kernel, [shape(16, 64, 128)], [whole()] * 2, flops=2 * 512 * 1024 * 256, moved=2 * MIB
    )(upstream, out_here)
    grads_own = lax.all_to_all(grad_send, PLANE, 0, 0, tiled=True)
    grads_other = swap(grads_own, "core")

    hidden_full = hidden.astype(F32)
    xhat, _ = normalized(hidden_full)
    normed_mlp = (xhat * m_gain + m_shift).astype(BF)
    inner = mm(normed_mlp, in_here) + in_bias_here
    bell = 0.5 * (1.0 + lax.erf(inner * (2.0**-0.5)))
    active = (inner * bell).astype(BF)
    proj_here = lax.dynamic_slice(proj_weight, (xl * 1024, 0), (1024, 1024))
    branch_mlp = mm(active, proj_here)
    active_grad = mm(upstream, proj_here, NT)
    slope = bell + inner * jnp.exp(-0.5 * inner * inner) * (1.0 / math.sqrt(2.0 * math.pi))
    inner_grad = (active_grad * slope).astype(BF)
    normed_mlp_grad = mm(inner_grad, in_here, NT)

    core_at = core.astype(jnp.int32).reshape(1)
    feed_own, feed_other = call(
        feed_weights_kernel,
        [shape(16, 512, 128)] * 2,
        [smem] + [whole()] * 4,
        flops=4 * 512 * 1024 * 1024,
        moved=8 * MIB,
    )(core_at, normed_mlp, inner_grad, active, upstream)

    def reduce_plane(own, other):
        both = own + swap(other, "core")
        parts = lax.all_to_all(both, PLANE, 0, 0, tiled=True)
        return jnp.sum(parts.astype(F32), axis=0).astype(BF)

    feed = reduce_plane(feed_own, feed_other)
    in_part = lax.all_to_all(
        jnp.broadcast_to(feed[:256].reshape(2, 1, 128, 128), (2, 2, 128, 128)).reshape(4, 128, 128),
        RING, 0, 0, tiled=True,
    )
    proj_part = in_order(xl == 0, feed[256:], swap(feed[256:], "xl"))
    feed_all = to_all(
        jnp.concatenate([in_part.reshape(512, 128), proj_part.reshape(512, 128)]), PLANE, 16
    )
    feed_core = swap(feed_all, "core")

    quarter = (group % 2) * 2 + core
    here = lax.dynamic_index_in_dim(doc_bounds, group // 8, 0, keepdims=False)
    place = jnp.concatenate([core_at, quarter.astype(jnp.int32).reshape(1), here])
    back_own, back_other = call(
        attend_kernel,
        [shape(16, 320, 128)] * 2,
        [smem, smem] + [whole()] * 4,
        scratch=[
            pltpu.VMEM((8192, 128), BF),
            pltpu.VMEM((128, 8192), BF),
            pltpu.VMEM((2048, 128), BF),
            pltpu.VMEM((128, 8192), F32),
            pltpu.VMEM((128, 8192), BF),
            pltpu.VMEM((128, 8192), F32),
            pltpu.VMEM((2048, 128), BF),
        ],
        flops=2 * 4 * 6 * 64 * 4 * MIB,
        moved=6 * MIB,
    )(place, block_map, heads_own, heads_other, grads_own, grads_other)

    arrived = swap(back_other, "core")
    returned = lax.all_to_all(
        jnp.concatenate(
            [back_own[:, :256] + arrived[:, :256], back_own[:, 256:], arrived[:, 256:]], axis=1
        ),
        PLANE, 0, 0, tiled=True,
    )
    project_grad, mixed = call(
        collect_kernel,
        [shape(512, 768), shape(512, 256)],
        [smem] + [whole()] * 3,
        scratch=[pltpu.VMEM((2, 128, 128), BF)],
        moved=3 * MIB,
    )(core_at, returned, cosine, sine)

    heads_grad_own, heads_grad_other = call(
        attend_weights_kernel,
        [shape(16, 256, 128)] * 2,
        [smem] + [whole()] * 4,
        flops=2 * 512 * 1024 * 1024,
        moved=6 * MIB,
    )(core_at, normed, project_grad, mixed, upstream)
    heads_sum = reduce_plane(heads_grad_own, heads_grad_other)
    qkv_part = lax.all_to_all(
        jnp.broadcast_to(heads_sum[:192].reshape(2, 1, 96, 128), (2, 2, 96, 128)).reshape(4, 96, 128),
        RING, 0, 0, tiled=True,
    )
    out_part = in_order(xl == 0, heads_sum[192:], swap(heads_sum[192:], "xl"))
    heads_all = to_all(
        jnp.concatenate([qkv_part.reshape(384, 128), out_part.reshape(128, 128)]), PLANE, 16
    )
    heads_core = swap(heads_all, "core")

    branch = branch_mlp + mm(mixed, out_here)
    normed_grad = mm(project_grad, qkv_here, NT)
    entry = normed_grad * a_gain + normed_mlp_grad * m_gain
    ring_rows = lax.all_to_all(
        jnp.concatenate([branch.reshape(4, 128, 1024), entry.reshape(4, 128, 1024)], axis=1).astype(BF),
        RING, 0, 0, tiled=True,
    )
    ring_rows = jnp.sum(ring_rows.astype(F32), axis=0)
    own_hidden = hidden_in[0].astype(F32)
    own_upstream = cotangent[0].astype(F32)
    hidden_out = (own_hidden + ring_rows[:128] + branch_bias).astype(BF)[None]
    own_xhat, own_scale = normalized(own_hidden)
    own_entry = ring_rows[128:]
    hidden_grad = (
        own_upstream
        + own_scale
        * (
            own_entry
            - jnp.mean(own_entry, axis=1, keepdims=True)
            - own_xhat * jnp.mean(own_entry * own_xhat, axis=1, keepdims=True)
        )
    )[None]

    def column_sum(array_in):
        return jnp.sum(array_in.astype(F32), axis=0)

    small = jnp.concatenate(
        [
            column_sum(normed_grad * xhat),
            column_sum(normed_grad),
            column_sum(normed_mlp_grad * xhat),
            column_sum(normed_mlp_grad),
            column_sum(own_upstream),
            column_sum(project_grad),
            column_sum(inner_grad),
            jnp.zeros((256,), F32),
        ]
    ).reshape(56, 128)
    small = small + swap(small, "core")
    small = jnp.sum(to_all(small, PLANE, 16), axis=0)
    small = to_all(small, RING, 4)
    common = jnp.sum(small[:, :40], axis=0).reshape(5, 1024)
    common = lax.dynamic_slice(common, (0, xh * 512), (5, 512))
    qkv_bias_grad = small[:, 40:46].reshape(4, 3, 256).transpose(1, 0, 2).reshape(3072)
    qkv_bias_grad = lax.dynamic_slice(qkv_bias_grad, (xh * 1536,), (1536,))
    in_bias_grad = lax.dynamic_slice(small[:, 46:54].reshape(4096), (xh * 2048,), (2048,))

    qkv_columns = [
        ((n // 2) * 1024 + c * 256 + (n % 2) * 128, c, n * 16, 16) for c in range(4) for n in range(6)
    ]
    in_columns = [(c * 1024 + n * 128, c, n * 16, 16) for c in range(4) for n in range(8)]

    def pieces(gathered, first_row, rows, chips):
        return gathered[:, first_row : first_row + rows].reshape(16, chips, rows // chips, 128)

    qkv_weight_grad = spread(
        core_at, pieces(heads_all, 0, 384, 4), pieces(heads_core, 0, 384, 4), 16, 3072, qkv_columns
    )
    in_weight_grad = spread(
        core_at, pieces(feed_all, 0, 512, 4), pieces(feed_core, 0, 512, 4), 16, 4096, in_columns
    )
    proj_own = pieces(feed_all, 512, 512, 2)
    proj_core = pieces(feed_core, 512, 512, 2)
    proj_both = in_order(core == 0, proj_own, proj_core).reshape(2, 16, 2, 8, 32, 128)
    proj_weight_grad = proj_both.transpose(2, 0, 1, 4, 3, 5).reshape(2048, 1024).astype(F32)
    out_own = pieces(heads_all, 384, 128, 2)
    out_core = pieces(heads_core, 384, 128, 2)
    out_both = in_order(core == 0, out_own, out_core).reshape(2, 16, 2, 4, 16, 128)
    out_weight_grad = out_both.transpose(2, 1, 4, 0, 3, 5).reshape(512, 1024).astype(F32)

    return (
        hidden_out, hidden_grad, common[0], common[1], common[2], common[3], qkv_weight_grad,
        qkv_bias_grad, out_weight_grad, common[4], in_weight_grad, in_bias_grad, proj_weight_grad,
        common[4],
    )


def solution(mesh):
    fine = Mesh(mesh.devices.reshape(4, 4, 2, 2, 2), ("y", "z", "xl", "core", "xh"))
    ctx = ("y", "z", "xl", "core")
    rows = P("xh", ctx, None)
    half = P("xh")
    wide = P("xh", None)
    in_specs = (
        rows, wide, P(), half, half, half, half, wide, half, wide, half, wide, half, wide, half, rows,
    )
    out_specs = (
        rows, rows, half, half, half, half, wide, half, wide, half, wide, half, wide, half,
    )
    return jax.shard_map(
        per_device, mesh=fine, in_specs=in_specs, out_specs=out_specs, check_vma=False
    )
```

```python
import functools
import math

import jax
import jax.numpy as jnp
from jax import lax
from jax.experimental import pallas as pl
from jax.experimental.pallas import tpu as pltpu
from jax.sharding import Mesh
from jax.sharding import PartitionSpec as P

ROT = 16
EPS = 1e-05
NEG_FILL = -1e30
BF = jnp.bfloat16
F32 = jnp.float32
RING = ("xh", "xl")
PLANE = ("y", "z")
MIB = 1 << 20

NN = (((1,), (0,)), ((), ()))
NT = (((1,), (1,)), ((), ()))
TN = (((0,), (0,)), ((), ()))


def mm(left, right, dims=NN):
    return lax.dot_general(left, right, dims, preferred_element_type=F32)


def mult(value, step):
    return pl.multiple_of(value, step)


def whole(space=pltpu.VMEM):
    return pl.BlockSpec(memory_space=space)


def call(body, outs, ins, scratch=(), flops=0, moved=0, limit=48):
    return pl.pallas_call(
        body,
        out_shape=outs,
        in_specs=ins,
        out_specs=[whole() for _ in outs],
        scratch_shapes=list(scratch),
        cost_estimate=pl.CostEstimate(flops=flops, bytes_accessed=moved, transcendentals=0),
        compiler_params=pltpu.CompilerParams(vmem_limit_bytes=limit * MIB),
    )


def to_all(array_in, axes, count):
    copies = jnp.broadcast_to(array_in[None], (count,) + array_in.shape)
    return lax.all_to_all(copies, axes, 0, 0, tiled=True)


def swap(array_in, axis):
    return lax.ppermute(array_in, axis, [(0, 1), (1, 0)])


def shift_ring(array_in, places):
    spots = [(x % 2) * 2 + x // 2 for x in range(4)]
    return lax.ppermute(
        array_in, ("xl", "xh"), [(spots[x], spots[(x + places) % 4]) for x in range(4)]
    )


def in_order(first, mine, other):
    return jnp.where(first, jnp.stack([mine, other]), jnp.stack([other, mine]))


def turn(tile, cosine, sine_low, sine_high):
    return (
        tile * cosine
        + pltpu.roll(tile, 120, 1) * sine_low
        + pltpu.roll(tile, 8, 1) * sine_high
    )


def sine_parts(sine, sign):
    spot = lax.broadcasted_iota(jnp.int32, sine.shape, 1) % 64
    low = jnp.where(spot < 8, -sign * sine, 0.0)
    high = jnp.where((spot >= 8) & (spot < 16), sign * sine, 0.0)
    return low, high


def project_kernel(
    place, rows0, rows1, rows2, rows3, gain, shift, mlp_gain, mlp_shift, weight_own, weight_other,
    bias, out_weight, cosine, sine, send, normed, normed_mlp, xhat, upstream,
):
    chip, half_in = place[1], place[2]
    here = pl.ds(mult(half_in * 512, 512), 512)
    there = pl.ds(mult(512 - half_in * 512, 512), 512)
    left = lax.broadcasted_iota(jnp.int32, (64, 128), 1) < 64
    left_all = lax.broadcasted_iota(jnp.int32, (128, 128), 1) < 64

    def pack(tile):
        low, high = tile[:64], tile[64:]
        return (
            jnp.where(left, low, pltpu.roll(high, 64, 1)).astype(BF),
            jnp.where(left, pltpu.roll(low, 64, 1), high).astype(BF),
        )

    for back, source in enumerate((rows0, rows1, rows2, rows3)):
        origin = (chip + 4 - back) % 4
        stream, half_x = origin // 2, origin % 2
        rows = pl.ds(back * 128, 128)
        moved = source[0].astype(F32)
        moved = moved - jnp.mean(moved, axis=1, keepdims=True)
        spread = jnp.mean(moved * moved, axis=1, keepdims=True)
        unit = moved * lax.rsqrt(spread + EPS)
        xhat[rows, :] = unit.astype(BF)
        normed[rows, :] = (unit * gain[...] + shift[...]).astype(BF)
        normed_mlp[rows, :] = (unit * mlp_gain[...] + mlp_shift[...]).astype(BF)
        upstream[rows, :] = source[1]
        project = (
            mm(normed[rows, here], weight_own[...]) + mm(normed[rows, there], weight_other[...]) + bias[...]
        )
        grads = mm(source[1], out_weight[...], NT)
        cos = cosine[rows, :]
        low, high = sine_parts(sine[rows, :], 1.0)
        for pair in range(2):
            at = pair * 128
            query = pack(turn(project[:, at : at + 128], cos, low, high) * 0.125)
            grad = pack(grads[:, at : at + 128])
            key = turn(project[:, 256 + at : 384 + at], cos, low, high)
            value = project[:, 512 + at : 640 + at]
            key_value = (
                jnp.where(left_all, key, pltpu.roll(value, 64, 1)).astype(BF),
                jnp.where(left_all, pltpu.roll(key, 64, 1), value).astype(BF),
            )
            for member in range(2):
                for half in range(2):
                    target = stream * 8 + (pair * 2 + member) * 2 + half
                    send[target, pl.ds(mult(half_x * 128, 128), 128), :] = key_value[member]
                    for core in range(2):
                        quarter = half * 2 + core
                        cut = slice(quarter * 16, quarter * 16 + 16)
                        spot = core * 32 + half_x * 16
                        send[target, pl.ds(mult(256 + spot, 16), 16), :] = query[member][cut]
                        send[target, pl.ds(mult(320 + spot, 16), 16), :] = grad[member][cut]


ROWS = 256
KEYS = 1024
SPAN = ROWS * 4
TILES = 8192 // SPAN
DIAGONAL = SPAN // KEYS


def attend_kernel(
    place, block_map, own, other, out_own, out_other,
    kv, kv_turned, q_grad, scores, chances, key_sums, rows_out,
):
    core, quarter, second, third = place[0], place[1], place[2], place[3]
    left16 = lax.broadcasted_iota(jnp.int32, (16, 128), 1) < 64
    left = lax.broadcasted_iota(jnp.int32, (ROWS, 128), 1) < 64
    def fill(source, from_core):
        @pl.loop(0, 32)
        def _(i):
            group, half_x = i // 2, i % 2
            block = block_map[i * 2 + from_core]
            mirror = 127 - block
            kv[pl.ds(mult(block * 64, 64), 64), :] = source[group, pl.ds(mult(half_x * 128, 64), 64), :]
            kv[pl.ds(mult(mirror * 64, 64), 64), :] = source[group, pl.ds(mult(half_x * 128 + 64, 64), 64), :]
            spot = core * 32 + half_x * 16
            query = source[group, pl.ds(mult(256 + spot, 16), 16), :].astype(F32)
            grad = source[group, pl.ds(mult(320 + spot, 16), 16), :].astype(F32)
            q_grad[pl.ds(mult(block * 16, 16), 16), :] = jnp.where(left16, query, pltpu.roll(grad, 64, 1)).astype(BF)
            q_grad[pl.ds(mult(mirror * 16, 16), 16), :] = jnp.where(left16, pltpu.roll(query, 64, 1), grad).astype(BF)
    fill(own, core)
    fill(other, 1 - core)
    @pl.loop(0, 16)
    def _(c):
        for d in range(4):
            cut = pl.ds(mult(c * 512 + d*128, 128), 128)
            kv_turned[:, cut] = kv[cut, :].astype(F32).T.astype(BF)
            key_sums[:, cut] = jnp.zeros((128, 128), F32)
    row = lax.broadcasted_iota(jnp.int32, (ROWS, 1), 0)
    offset = (row // 16) * 64 + quarter * 16 + row % 16
    spots = lax.broadcasted_iota(jnp.int32, (ROWS, KEYS), 1)
    def start_of(position):
        return jnp.where(position >= third, third, jnp.where(position >= second, second, 0))
    @pl.loop(0, TILES)
    def _(step):
        tile = TILES-1 - step
        rows = pl.ds(mult(tile * ROWS, ROWS), ROWS)
        base = tile * SPAN
        both = q_grad[rows, :]
        query, grad = both[:, :64], both[:, 64:]
        position = base + offset
        first = start_of(position)
        diag = tile * DIAGONAL
        low = start_of(base + quarter * 16) // KEYS
        high = (start_of(base + SPAN - 64 + quarter * 16 + 15) + KEYS - 1) // KEYS
        high = jnp.minimum(jnp.maximum(high, low), diag)
        low_ = jnp.minimum(low, diag)
        def cut_of(j):
            return pl.ds(mult(j * KEYS, KEYS), KEYS)
        def fold(top, part):
            for c in range(KEYS // 128):
                top = jnp.maximum(top, part[:, c * 128 : c * 128 + 128])
            return top
        def plain(j, top):
            part = mm(query, kv_turned[0:64, cut_of(j)])
            scores[:, cut_of(j)] = part
            return fold(top, part)
        def masked(j, top):
            part = mm(query, kv_turned[0:64, cut_of(j)])
            key_at = spots + j * KEYS
            part = jnp.where((key_at <= position) & (key_at >= first), part, NEG_FILL)
            scores[:, cut_of(j)] = part
            return fold(top, part)
        top = jnp.full((ROWS, 128), NEG_FILL, F32)
        top = lax.fori_loop(low_, high, masked, top)
        top = lax.fori_loop(high, diag, plain, top)
        for d in range(DIAGONAL):
            top = masked(diag + d, top)
        row_top = jnp.max(top, axis=1, keepdims=True)
        def weigh(j, state):
            total, mixed = state
            part = jnp.exp(scores[:, cut_of(j)] - row_top)
            for c in range(KEYS // 128):
                total = total + part[:, c * 128 : c * 128 + 128]
            rounded = part.astype(BF)
            chances[:, cut_of(j)] = rounded
            return total, mixed + mm(rounded, kv[cut_of(j), :])
        zero = jnp.zeros((ROWS, 128), F32)
        total, mixed = lax.fori_loop(low_, diag + DIAGONAL, weigh, (zero, zero))
        share = 1.0 / jnp.sum(total, axis=1, keepdims=True)
        mixed = mixed * share
        scaled = jnp.where(left, both.astype(F32), both.astype(F32) * share)
        delta = jnp.sum(jnp.where(left, 0.0, scaled * mixed), axis=1, keepdims=True)
        grad_scaled = scaled[:, 64:].astype(BF)
        turned = scaled.T.astype(BF)
        query_turned, grad_turned = turned[:64], turned[64:]
        def back(j, query_sum):
            cut = cut_of(j)
            part = chances[:, cut]
            along = mm(grad_scaled, kv_turned[64:128, cut])
            score_grad = (part.astype(F32) * (along - delta)).astype(BF)
            key_sums[0:64, cut] += mm(query_turned, score_grad)
            key_sums[64:128, cut] += mm(grad_turned, part)
            return query_sum + mm(score_grad, kv[cut, :])
        query_sum = lax.fori_loop(low_, diag + DIAGONAL, back, zero)
        rows_out[rows, :] = jnp.where(left, query_sum * 0.125, mixed).astype(BF)
    @pl.loop(0, 16)
    def _(c):
        for d in range(4):
            cut = pl.ds(mult(c * 512+d*128, 128), 128)
            kv[cut, :] = key_sums[:, cut].T.astype(BF)
    def spill(target, to_core):
        @pl.loop(0, 32)
        def _(i):
            group, half_x = i // 2, i % 2
            block = block_map[i * 2 + to_core]
            mirror = 127 - block
            target[group, pl.ds(mult(half_x * 128, 64), 64), :] = kv[pl.ds(mult(block * 64, 64), 64), :]
            target[group, pl.ds(mult(half_x * 128 + 64, 64), 64), :] = kv[pl.ds(mult(mirror * 64, 64), 64), :]
            spot = 256 + half_x * 32
            target[group, pl.ds(mult(spot, 16), 16), :] = rows_out[pl.ds(mult(block * 16, 16), 16), :]
            target[group, pl.ds(mult(spot + 16, 16), 16), :] = rows_out[pl.ds(mult(mirror * 16, 16), 16), :]
    spill(out_own, core)
    spill(out_other, 1 - core)


def return_kernel(
    place, back, cosine, sine, normed, xhat, upstream, weight, early,
    out_own, out_other, normed_grad, project_grad, mixed_out, heads, small,
):
    core, chip = place[0], place[1]
    left = lax.broadcasted_iota(jnp.int32, (128, 128), 1) < 64
    for behind in range(4):
        origin = (chip + 4 - behind) % 4
        stream, half_x = origin // 2, origin % 2
        rows = pl.ds(behind * 128, 128)
        cos = cosine[rows, :]
        low, high = sine_parts(sine[rows, :], -1.0)
        for pair in range(2):
            pieces = []
            for member in range(2):
                base = stream * 8 + (pair * 2 + member) * 2
                cut = pl.ds(mult(half_x * 128, 128), 128)
                key_value = back[base, cut, :].astype(F32) + back[base + 1, cut, :].astype(F32)
                for upper in range(2):
                    for half in range(2):
                        for of_core in range(2):
                            flipped = of_core ^ core
                            spot = 256 + flipped * 64 + (half_x * 2 + upper) * 16
                            heads[
                                member, pl.ds(upper * 64 + (half * 2 + of_core) * 16, 16), :
                            ] = back[base + half, pl.ds(mult(spot, 16), 16), :]
                pieces.append((heads[member].astype(F32), key_value))
            (row0, kv0), (row1, kv1) = pieces
            at = pair * 128
            query = jnp.where(left, row0, pltpu.roll(row1, 64, 1))
            key = jnp.where(left, kv0, pltpu.roll(kv1, 64, 1))
            value = jnp.where(left, pltpu.roll(kv0, 64, 1), kv1)
            mixed = jnp.where(left, pltpu.roll(row0, 64, 1), row1)
            project_grad[rows, at : at + 128] = turn(query, cos, low, high).astype(BF)
            project_grad[rows, 256 + at : 384 + at] = turn(key, cos, low, high).astype(BF)
            project_grad[rows, 512 + at : 640 + at] = value.astype(BF)
            mixed_out[rows, at : at + 128] = mixed.astype(BF)

    small[...] = jnp.zeros_like(small)
    for k in range(32):
        small[0, k // 2, k % 2 : k % 2 + 1, :] = early[k : k + 1, :]

    def keep(first, sums):
        for n in range(sums.shape[1] // 128):
            k = first + n
            small[1, k // 2, k % 2 : k % 2 + 1, :] = sums[:, n * 128 : n * 128 + 128]

    gain_sums = jnp.zeros((1, 1024), F32)
    shift_sums = jnp.zeros((1, 1024), F32)
    bias_sums = jnp.zeros((1, 768), F32)
    for block in range(4):
        rows = pl.ds(block * 128, 128)
        grads = project_grad[rows, :]
        entry = mm(grads, weight[...], NT)
        normed_grad[rows, :] = entry
        gain_sums += jnp.sum(entry * xhat[rows, :].astype(F32), axis=0, keepdims=True)
        shift_sums += jnp.sum(entry, axis=0, keepdims=True)
        bias_sums += jnp.sum(grads.astype(F32), axis=0, keepdims=True)
    keep(0, gain_sums)
    keep(8, shift_sums)
    keep(16, bias_sums)

    for flip, target in ((0, out_own), (1, out_other)):
        to_core = core ^ flip
        for part in range(2):
            columns = normed[:, pl.ds(mult(part * 512 + to_core * 256, 256), 256)]
            for block in range(3):
                grads = mm(columns, project_grad[:, block * 256 : block * 256 + 256], TN).astype(BF)
                for n in range(2):
                    slot = part * 6 + block * 2 + n
                    target[:, slot * 16 : slot * 16 + 16, :] = grads[:, n * 128 : n * 128 + 128].reshape(
                        16, 16, 128
                    )
        for block in range(2):
            columns = upstream[:, pl.ds(mult(to_core * 512 + block * 256, 256), 256)]
            grads = mm(mixed_out[...], columns, TN).astype(BF)
            for n in range(2):
                at = 192 + (block * 2 + n) * 16
                target[:, at : at + 16, :] = grads[:, n * 128 : n * 128 + 128].reshape(16, 16, 128)
        target[:, 256:272, :] = small[to_core].astype(BF)


def feed_weights_kernel(place, normed, inner_grad, active, upstream, out_own, out_other):
    for flip, target in ((0, out_own), (1, out_other)):
        core = place[0] ^ flip
        for part in range(2):
            rows = normed[:, pl.ds(mult(part * 512 + core * 256, 256), 256)]
            for quad in range(4):
                grads = mm(rows, inner_grad[:, quad * 256 : quad * 256 + 256], TN).astype(BF)
                for n in range(2):
                    slot = part * 8 + quad * 2 + n
                    target[:, slot * 16 : slot * 16 + 16, :] = grads[:, n * 128 : n * 128 + 128].reshape(
                        16, 16, 128
                    )
        rows = active[:, pl.ds(mult(core * 512, 512), 512)]
        for quad in range(4):
            grads = mm(rows, upstream[:, quad * 256 : quad * 256 + 256], TN).astype(BF)
            for n in range(2):
                at = 256 + (quad * 2 + n) * 32
                target[:, at : at + 32, :] = grads[:, n * 128 : n * 128 + 128].reshape(16, 32, 128)


def spread_kernel(place, piece, out, *, columns):
    for behind, slot, rows, step, at in columns:
        start = at
        if step:
            start = mult(at + ((place[1] + 4 - behind) % 4) * step, 128)
        out[:, pl.ds(start, 128)] = piece[0, slot : slot + rows, :].astype(F32)


def spread(place, pieces, shape_out, block, at_row, grid, in_map, out_map, columns):
    height, width = block
    return pl.pallas_call(
        functools.partial(spread_kernel, columns=columns),
        out_shape=jax.ShapeDtypeStruct(shape_out, F32),
        grid_spec=pltpu.PrefetchScalarGridSpec(
            num_scalar_prefetch=1,
            grid=grid,
            in_specs=[pl.BlockSpec((1, at_row, 128), in_map)],
            out_specs=pl.BlockSpec((height, width), out_map),
        ),
        cost_estimate=pl.CostEstimate(
            flops=0, bytes_accessed=shape_out[0] * shape_out[1] * 6, transcendentals=0
        ),
        compiler_params=pltpu.CompilerParams(vmem_limit_bytes=32 * MIB),
    )(place, pieces)


def shape(*sizes, dtype=BF):
    return jax.ShapeDtypeStruct(sizes, dtype)


def normalized(hidden):
    moved = hidden - jnp.mean(hidden, axis=-1, keepdims=True)
    spread_out = jnp.mean(moved * moved, axis=-1, keepdims=True)
    scale = lax.rsqrt(spread_out + EPS)
    return moved * scale, scale


def per_device(
    hidden_in, doc_ids, block_map, attn_gain, attn_shift, mlp_gain, mlp_shift, qkv_weight, qkv_bias,
    out_weight, out_bias, in_weight, in_bias, proj_weight, proj_bias, cotangent,
):
    y, z = lax.axis_index("y"), lax.axis_index("z")
    xh, xl = lax.axis_index("xh"), lax.axis_index("xl")
    core = lax.axis_index("core")
    group = y * 4 + z
    chip = xh * 2 + xl
    low_half = xh == 0
    smem = whole(pltpu.SMEM)
    place = jnp.stack([core, chip, xh, xl]).astype(jnp.int32)

    payload = jnp.stack([hidden_in[0], cotangent[0]])
    ring = [payload] + [shift_ring(payload, d) for d in (1, 2, 3)]
    origins = (chip + 4 - jnp.arange(4, dtype=jnp.int32)) % 4

    partner = (1 - xh) * 2 + xl

    def qkv_columns_of(which, first_row, rows):
        return jnp.concatenate(
            [lax.dynamic_slice(qkv_weight, (first_row, k * 1024 + which * 256), (rows, 256)) for k in range(3)],
            axis=1,
        )

    piece = swap(qkv_columns_of(partner, group * 32, 32), "xh")
    qkv_other = to_all(piece, PLANE, 16).reshape(512, 768)
    qkv_own = qkv_columns_of(chip, 0, 512)
    piece = swap(lax.dynamic_slice(in_weight, (core * 256, partner * 1024), (256, 1024)), "xh")
    in_other = in_order(core == 0, piece, swap(piece, "core")).reshape(512, 1024)
    in_own = lax.dynamic_slice(in_weight, (0, chip * 1024), (512, 1024))

    segment = doc_ids[0]
    bounds = jnp.stack([jnp.sum((segment < label).astype(jnp.int32)) for label in (1, 2)])
    bound_parts = jnp.stack([bounds // 128, bounds % 128]).reshape(4).astype(BF)
    vectors = jnp.concatenate(
        [attn_gain, attn_shift, mlp_gain, mlp_shift, qkv_bias, in_bias, out_bias, proj_bias,
         bound_parts, jnp.zeros((508,), BF)]
    ).reshape(56, 128)
    vectors_other = swap(vectors, "xh")
    pairs = in_order(low_half, vectors.reshape(-1), vectors_other.reshape(-1))
    a_gain = pairs[:, 0:512].reshape(1, 1024).astype(F32)
    a_shift = pairs[:, 512:1024].reshape(1, 1024).astype(F32)
    m_gain = pairs[:, 1024:1536].reshape(1, 1024).astype(F32)
    m_shift = pairs[:, 1536:2048].reshape(1, 1024).astype(F32)
    qkv_bias_all = pairs[:, 2048:3584].reshape(3, 1024).astype(F32)
    qkv_bias_here = lax.dynamic_slice(qkv_bias_all, (0, chip * 256), (3, 256)).reshape(1, 768)
    in_bias_here = lax.dynamic_slice(
        pairs[:, 3584:5632].reshape(1, 4096), (0, chip * 1024), (1, 1024)
    ).astype(F32)
    branch_bias = (
        pairs[:, 5632:6144].reshape(1, 1024).astype(F32) + pairs[:, 6144:6656].reshape(1, 1024).astype(F32)
    )
    bound_pairs = pairs[:, 6656:6660].astype(F32).astype(jnp.int32)
    doc_bounds = bound_pairs[:, 0:2] * 128 + bound_pairs[:, 2:4]

    blocks = jnp.take(block_map, (group * 2 + origins % 2) * 2 + core)[:, None]
    steps = jnp.arange(64, dtype=jnp.int32)[None]
    position = jnp.concatenate([blocks * 64 + steps, (127 - blocks) * 64 + steps], axis=1)
    row_bounds = jnp.take(doc_bounds, origins // 2, axis=0)
    second, third = row_bounds[:, 0:1], row_bounds[:, 1:2]
    first = jnp.where(position >= third, third, jnp.where(position >= second, second, 0))
    relative = (position - first).astype(F32).reshape(512, 1)
    frequency = 10000.0 ** (-(jnp.arange(0, ROT, 2).astype(F32) / ROT))
    lanes = jnp.concatenate([frequency, frequency, jnp.zeros((48,), F32)])
    angles = relative * jnp.concatenate([lanes, lanes])[None]
    cosine, sine = jnp.cos(angles), jnp.sin(angles)

    out_here = lax.dynamic_slice(out_weight, (xl * 256, 0), (256, 1024))
    send, normed, normed_mlp, xhat, upstream = call(
        project_kernel,
        [shape(16, 384, 128)] + [shape(512, 1024)] * 4,
        [smem] + [whole()] * 14,
        flops=2 * 512 * 1024 * 1024,
        moved=12 * MIB,
    )(place, *ring, a_gain, a_shift, m_gain, m_shift, qkv_own, qkv_other, qkv_bias_here, out_here,
      cosine, sine)
    heads_own = lax.all_to_all(send, PLANE, 0, 0, tiled=True)
    heads_other = swap(heads_own, "core")

    in_here = in_order(low_half, in_own, in_other).reshape(1024, 1024)
    inner = mm(normed_mlp, in_here) + in_bias_here
    bell = 0.5 * (1.0 + lax.erf(inner * (2.0**-0.5)))
    active = (inner * bell).astype(BF)
    proj_here = lax.dynamic_slice(proj_weight, (xl * 1024, 0), (1024, 1024))
    branch_mlp = mm(active, proj_here)
    active_grad = mm(upstream, proj_here, NT)
    slope = bell + inner * jnp.exp(-0.5 * inner * inner) * (1.0 / math.sqrt(2.0 * math.pi))
    inner_grad = (active_grad * slope).astype(BF)
    normed_mlp_grad = mm(inner_grad, in_here, NT)

    def column_sum(array_in):
        return jnp.sum(array_in.astype(F32), axis=0)

    early = jnp.concatenate(
        [
            column_sum(normed_mlp_grad * xhat.astype(F32)),
            column_sum(normed_mlp_grad),
            column_sum(cotangent[0]),
            column_sum(inner_grad),
        ]
    ).reshape(32, 128)
    entry_mlp = normed_mlp_grad * m_gain

    feed_own, feed_other = call(
        feed_weights_kernel,
        [shape(16, 512, 128)] * 2,
        [smem] + [whole()] * 4,
        flops=4 * 512 * 1024 * 1024,
        moved=8 * MIB,
    )(place, normed_mlp, inner_grad, active, upstream)
    feed_both = feed_own + swap(feed_other, "core")

    def reduce_plane(both):
        parts = lax.all_to_all(both, PLANE, 0, 0, tiled=True)
        return jnp.sum(parts.astype(F32), axis=0).astype(BF)

    def around(parts, rest=()):
        got = [jnp.concatenate([lax.dynamic_index_in_dim(parts, xh, 0, False), *rest])]
        for d in (1, 2, 3):
            half = ((chip + d) % 4) // 2
            got.append(
                shift_ring(jnp.concatenate([lax.dynamic_index_in_dim(parts, half, 0, False), *rest]), d)
            )
        return got

    heads_own, heads_other, feed_both, early, entry_mlp, branch_mlp = lax.optimization_barrier(
        (heads_own, heads_other, feed_both, early, entry_mlp, branch_mlp)
    )
    feed = reduce_plane(feed_both)
    quarter = (group % 2) * 2 + core
    bounds_here = lax.dynamic_index_in_dim(doc_bounds, group // 8, 0, keepdims=False)
    spot = jnp.concatenate([jnp.stack([core, quarter]).astype(jnp.int32), bounds_here])
    back_own, back_other = call(
        attend_kernel,
        [shape(16, 320, 128)] * 2,
        [smem, smem] + [whole()] * 2,
        scratch=[
            pltpu.VMEM((8192, 128), BF),
            pltpu.VMEM((128, 8192), BF),
            pltpu.VMEM((2048, 128), BF),
            pltpu.VMEM((ROWS, 8192), F32),
            pltpu.VMEM((ROWS, 8192), BF),
            pltpu.VMEM((128, 8192), F32),
            pltpu.VMEM((2048, 128), BF),
        ],
        flops=45 * 10**9,
        moved=6 * MIB,
    )(spot, block_map, heads_own, heads_other)

    arrived = swap(back_other, "core")
    returned = lax.all_to_all(
        jnp.concatenate(
            [back_own[:, :256] + arrived[:, :256], back_own[:, 256:], arrived[:, 256:]], axis=1
        ),
        PLANE, 0, 0, tiled=True,
    )

    feed, back_own = lax.optimization_barrier((feed, back_own))
    in_parts = around(feed[:256].reshape(2, 128, 128))
    feed_all = lax.all_gather(
        jnp.concatenate(in_parts + [feed[256:], swap(feed[256:], "xl")]), ("core",) + PLANE, axis=0
    )

    qkv_here = in_order(low_half, qkv_own, qkv_other).reshape(1024, 768)
    heads_grad_own, heads_grad_other, normed_grad, project_grad, mixed = call(
        return_kernel,
        [shape(16, 272, 128)] * 2 + [shape(512, 1024, dtype=F32), shape(512, 768), shape(512, 256)],
        [smem] + [whole()] * 8,
        scratch=[pltpu.VMEM((2, 128, 128), BF), pltpu.VMEM((2, 16, 16, 128), F32)],
        flops=4 * 512 * 1024 * 1024,
        moved=9 * MIB,
    )(place, returned, cosine, sine, normed, xhat, upstream, qkv_here, early)

    heads_sum = reduce_plane(heads_grad_own + swap(heads_grad_other, "core"))
    heads_parts = around(heads_sum[:192].reshape(2, 96, 128), (heads_sum[256:], heads_sum[192:256]))
    beside = jnp.where(xl == 0, heads_parts[3], heads_parts[1])
    heads_all = to_all(
        jnp.concatenate([part[:112] for part in heads_parts] + [heads_parts[0][112:], beside[112:]]),
        PLANE, 16,
    )
    heads_core = swap(heads_all, "core")

    branch = branch_mlp + mm(mixed, out_here)
    entry = normed_grad * a_gain + entry_mlp
    to_rows = jnp.concatenate([branch.reshape(4, 128, 1024), entry.reshape(4, 128, 1024)], axis=1).astype(BF)
    ring_rows = to_rows[0].astype(F32)
    for d in (1, 2, 3):
        ring_rows = ring_rows + shift_ring(to_rows[d], 4 - d).astype(F32)
    own_hidden = hidden_in[0].astype(F32)
    hidden_out = (own_hidden + ring_rows[:128] + branch_bias).astype(BF)[None]
    own_xhat, own_scale = normalized(own_hidden)
    own_entry = ring_rows[128:]
    hidden_grad = (
        cotangent[0].astype(F32)
        + own_scale
        * (
            own_entry
            - jnp.mean(own_entry, axis=1, keepdims=True)
            - own_xhat * jnp.mean(own_entry * own_xhat, axis=1, keepdims=True)
        )
    )[None]

    small = in_order(core == 0, heads_all[:, :448], heads_core[:, :448]).reshape(2, 16, 4, 112, 128)
    small = small[:, :, :, 96:98].astype(F32).transpose(2, 0, 1, 3, 4).reshape(4, 2, 4, 1024)
    common = jnp.sum(small, axis=0)
    in_order_of_chips = jnp.take(small, origins, axis=0)
    own_columns = lax.dynamic_slice(common, (0, 0, xh * 512), (2, 4, 512))
    in_bias_grad = lax.dynamic_slice(in_order_of_chips[:, 0, 3].reshape(4096), (xh * 2048,), (2048,))
    qkv_bias_grad = in_order_of_chips[:, 1, 2:].reshape(4, 2048)[:, :768].reshape(4, 3, 256)
    qkv_bias_grad = qkv_bias_grad.transpose(1, 0, 2).reshape(3072)
    qkv_bias_grad = lax.dynamic_slice(qkv_bias_grad, (xh * 1536,), (1536,))

    in_weight_grad = spread(
        place, feed_all, (512, 4096), (16, 4096), 512, (32,),
        lambda g, place: (g, 0, 0), lambda g, place: (g, 0),
        [(c, c * 128 + n * 16, 16, 1024, n * 128) for c in range(4) for n in range(8)],
    )
    proj_weight_grad = spread(
        place, feed_all, (2048, 1024), (32, 1024), 256, (2, 32),
        lambda a, g, place: (g, 2 + a, 0), lambda a, g, place: ((place[3] ^ a) * 32 + g, 0),
        [(0, n * 32, 32, 0, n * 128) for n in range(8)],
    )
    heads_full = in_order(core == 0, heads_all, heads_core).reshape(32, 576, 128)
    qkv_weight_grad = spread(
        place, heads_full, (512, 3072), (16, 3072), 576, (32,),
        lambda g, place: (g, 0, 0), lambda g, place: (g, 0),
        [
            (c, c * 112 + n * 16, 16, 256, (n // 2) * 1024 + (n % 2) * 128)
            for c in range(4)
            for n in range(6)
        ],
    )
    out_weight_grad = spread(
        place, heads_full, (512, 1024), (16, 512), 64, (2, 32),
        lambda a, g, place: (g, 7 + a, 0),
        lambda a, g, place: ((place[3] ^ a) * 16 + g % 16, g // 16),
        [(0, n * 16, 16, 0, n * 128) for n in range(4)],
    )

    return (
        hidden_out, hidden_grad, own_columns[1, 0], own_columns[1, 1], own_columns[0, 0],
        own_columns[0, 1], qkv_weight_grad, qkv_bias_grad, out_weight_grad, own_columns[0, 2],
        in_weight_grad, in_bias_grad, proj_weight_grad, own_columns[0, 2],
    )


def solution(mesh):
    fine = Mesh(mesh.devices.reshape(4, 4, 2, 2, 2), ("y", "z", "xl", "core", "xh"))
    ctx = ("y", "z", "xl", "core")
    rows = P("xh", ctx, None)
    half = P("xh")
    wide = P("xh", None)
    in_specs = (
        rows, wide, P(), half, half, half, half, wide, half, wide, half, wide, half, wide, half, rows,
    )
    out_specs = (
        rows, rows, half, half, half, half, wide, half, wide, half, wide, half, wide, half,
    )
    return jax.shard_map(
        per_device, mesh=fine, in_specs=in_specs, out_specs=out_specs, check_vma=False
    )
```

```python
import functools
import math

import jax
import jax.numpy as jnp
from jax import lax
from jax.experimental import pallas as pl
from jax.experimental.pallas import tpu as pltpu
from jax.sharding import Mesh
from jax.sharding import PartitionSpec as P

ROT = 16
EPS = 1e-05
NEG_FILL = -1e30
BF = jnp.bfloat16
F32 = jnp.float32
RING = ("xh", "xl")
PLANE = ("y", "z")
MIB = 1 << 20

NN = (((1,), (0,)), ((), ()))
NT = (((1,), (1,)), ((), ()))
TN = (((0,), (0,)), ((), ()))


def mm(left, right, dims=NN):
    return lax.dot_general(left, right, dims, preferred_element_type=F32)


def mult(value, step):
    return pl.multiple_of(value, step)


def whole(space=pltpu.VMEM):
    return pl.BlockSpec(memory_space=space)


def call(body, outs, ins, scratch=(), flops=0, moved=0, limit=60):
    return pl.pallas_call(
        body,
        out_shape=outs,
        in_specs=ins,
        out_specs=[whole() for _ in outs],
        scratch_shapes=list(scratch),
        cost_estimate=pl.CostEstimate(flops=flops, bytes_accessed=moved, transcendentals=0),
        compiler_params=pltpu.CompilerParams(vmem_limit_bytes=limit * MIB),
    )


def to_all(array_in, axes, count):
    copies = jnp.broadcast_to(array_in[None], (count,) + array_in.shape)
    return lax.all_to_all(copies, axes, 0, 0, tiled=True)


def swap(array_in, axis):
    return lax.ppermute(array_in, axis, [(0, 1), (1, 0)])


def shift_ring(array_in, places):
    spots = [(x % 2) * 2 + x // 2 for x in range(4)]
    return lax.ppermute(
        array_in, ("xl", "xh"), [(spots[x], spots[(x + places) % 4]) for x in range(4)]
    )


def in_order(first, mine, other):
    return jnp.where(first, jnp.stack([mine, other]), jnp.stack([other, mine]))


def turn(tile, cosine, sine_low, sine_high):
    return (
        tile * cosine
        + pltpu.roll(tile, 120, 1) * sine_low
        + pltpu.roll(tile, 8, 1) * sine_high
    )


def sine_parts(sine, sign):
    spot = lax.broadcasted_iota(jnp.int32, sine.shape, 1) % 64
    low = jnp.where(spot < 8, -sign * sine, 0.0)
    high = jnp.where((spot >= 8) & (spot < 16), sign * sine, 0.0)
    return low, high


def vector_kernel(*refs):
    docs, out = refs[-2], refs[-1]
    out[...] = jnp.zeros_like(out)
    row = 0
    for ref in refs[:-2]:
        for part in range(ref.shape[1] // 512):
            out[row : row + 1, :] = ref[:, part * 512 : part * 512 + 512].astype(F32)
            row += 1
    lane = lax.broadcasted_iota(jnp.int32, (1, 512), 1)
    counts = [
        jnp.sum(jnp.sum((docs[...] < label).astype(F32), axis=0, keepdims=True), axis=1, keepdims=True)
        for label in (1, 2)
    ]
    out[13:14, :] = jnp.where(lane == 0, counts[0], jnp.where(lane == 1, counts[1], 0.0))


def halves(half_in, core):
    start = 512 - half_in * 512
    return (
        pl.ds(mult(half_in * 512, 512), 512),
        pl.ds(mult(start + core * 256, 256), 256),
        pl.ds(mult(start + 256 - core * 256, 256), 256),
    )


def fetch(copies):
    started = [pltpu.make_async_copy(*copy) for copy in copies]
    for copy in started:
        copy.start()
    return started


def qkv_copies(weight, chip, target, sems):
    return [
        (
            weight.at[:, pl.ds(mult(k * 1024 + chip * 256, 256), 256)],
            target.at[:, pl.ds(k * 256, 256)],
            sems.at[k],
        )
        for k in range(3)
    ]


def project_kernel(
    place, block_map, rows0, rows1, rows2, rows3, vector, vector_other, lanes, weight, weight_mine,
    weight_other, out_weight, send, normed, normed_mlp, xhat, upstream, cosine, sine, gains,
    weight_here, out_here, sems,
):
    own_core, chip, half_in, low_x, group = place[0], place[1], place[2], place[3], place[4]
    here, mine, others = halves(half_in, own_core)
    copies = fetch(
        qkv_copies(weight, chip, weight_here, sems)
        + [(out_weight.at[pl.ds(mult(low_x * 256, 256), 256), :], out_here, sems.at[3])]
    )
    there = pl.ds(mult(512 - half_in * 512, 512), 512)
    for k in range(4):
        gains[k : k + 1, here] = vector[k : k + 1, :]
        gains[k : k + 1, there] = vector_other[k : k + 1, :]
    left = lax.broadcasted_iota(jnp.int32, (64, 128), 1) < 64
    left_all = lax.broadcasted_iota(jnp.int32, (128, 128), 1) < 64
    row = lax.broadcasted_iota(jnp.int32, (128, 1), 0)

    def pack(tile):
        low, high = tile[:64], tile[64:]
        return (
            jnp.where(left, low, pltpu.roll(high, 64, 1)).astype(BF),
            jnp.where(left, pltpu.roll(low, 64, 1), high).astype(BF),
        )

    def bias_of(k):
        at = k * 1024 + chip * 256
        inside = at % 1536
        spot = (pl.ds(4 + inside // 512, 1), pl.ds(mult(inside % 512, 256), 256))
        return jnp.where(at // 1536 == half_in, vector[spot], vector_other[spot])

    biases = [bias_of(k) for k in range(3)]
    for copy in copies:
        copy.wait()
    for back, source in enumerate((rows0, rows1, rows2, rows3)):
        origin = (chip + 4 - back) % 4
        stream, half_x = origin // 2, origin % 2
        rows = pl.ds(back * 128, 128)
        moved = source[0].astype(F32)
        moved = moved - jnp.mean(moved, axis=1, keepdims=True)
        spread = jnp.mean(moved * moved, axis=1, keepdims=True)
        unit = moved * lax.rsqrt(spread + EPS)
        xhat[rows, :] = unit.astype(BF)
        normed[rows, :] = (unit * gains[0:1, :] + gains[1:2, :]).astype(BF)
        normed_mlp[rows, :] = (unit * gains[2:3, :] + gains[3:4, :]).astype(BF)
        upstream[rows, :] = source[1]

        block = block_map[(group * 2 + half_x) * 2 + own_core]
        position = jnp.where(row < 64, block * 64 + row, (127 - block) * 64 + row - 64).astype(F32)
        same = stream == half_in
        second = jnp.where(same, vector[13:14, 0:1], vector_other[13:14, 0:1])
        third = jnp.where(same, vector[13:14, 1:2], vector_other[13:14, 1:2])
        first = jnp.where(position >= third, third, jnp.where(position >= second, second, 0.0))
        angles = (position - first) * lanes[...]
        cos, sin = jnp.cos(angles), jnp.sin(angles)
        cosine[rows, :] = cos
        sine[rows, :] = sin
        low, high = sine_parts(sin, 1.0)

        def project(k):
            columns = slice(k * 256, k * 256 + 256)
            return (
                mm(normed[rows, here], weight_here[:, columns])
                + mm(normed[rows, mine], weight_mine[:, columns])
                + mm(normed[rows, others], weight_other[:, columns])
                + biases[k]
            )

        queries, keys, values = project(0), project(1), project(2)
        grads = mm(source[1], out_here[...], NT)
        for pair in range(2):
            at = pair * 128
            query = pack(turn(queries[:, at : at + 128], cos, low, high) * 0.125)
            grad = pack(grads[:, at : at + 128])
            key = turn(keys[:, at : at + 128], cos, low, high)
            value = values[:, at : at + 128]
            key_value = (
                jnp.where(left_all, key, pltpu.roll(value, 64, 1)).astype(BF),
                jnp.where(left_all, pltpu.roll(key, 64, 1), value).astype(BF),
            )
            for member in range(2):
                for half in range(2):
                    target = stream * 8 + (pair * 2 + member) * 2 + half
                    send[target, pl.ds(mult(half_x * 128, 128), 128), :] = key_value[member]
                    for core in range(2):
                        quarter = half * 2 + core
                        cut = slice(quarter * 16, quarter * 16 + 16)
                        spot = core * 32 + half_x * 16
                        send[target, pl.ds(mult(256 + spot, 16), 16), :] = query[member][cut]
                        send[target, pl.ds(mult(320 + spot, 16), 16), :] = grad[member][cut]


ROWS = 256
KEYS = 1024


def attend_kernel(
    place, block_map, own, other, out_own, out_other, kv, q_grad, scores, chances, key_sums, rows_out,
):
    core, quarter, second, third = place[0], place[1], place[2], place[3]
    left16 = lax.broadcasted_iota(jnp.int32, (16, 128), 1) < 64
    left = lax.broadcasted_iota(jnp.int32, (ROWS, 128), 1) < 64

    def fill(source, from_core):
        @pl.loop(0, 8)
        def _(step):
            for unrolled in range(4):
                i = step * 4 + unrolled
                group, half_x = i // 2, i % 2
                block = block_map[i * 2 + from_core]
                mirror = 127 - block
                kv[pl.ds(mult(block * 64, 64), 64), :] = source[
                    group, pl.ds(mult(half_x * 128, 64), 64), :
                ]
                kv[pl.ds(mult(mirror * 64, 64), 64), :] = source[
                    group, pl.ds(mult(half_x * 128 + 64, 64), 64), :
                ]
                spot = core * 32 + half_x * 16
                query = source[group, pl.ds(mult(256 + spot, 16), 16), :].astype(F32)
                grad = source[group, pl.ds(mult(320 + spot, 16), 16), :].astype(F32)
                q_grad[pl.ds(mult(block * 16, 16), 16), :] = jnp.where(
                    left16, query, pltpu.roll(grad, 64, 1)
                ).astype(BF)
                q_grad[pl.ds(mult(mirror * 16, 16), 16), :] = jnp.where(
                    left16, pltpu.roll(query, 64, 1), grad
                ).astype(BF)

    fill(own, core)
    fill(other, 1 - core)
    key_sums[...] = jnp.zeros_like(key_sums)

    row = lax.broadcasted_iota(jnp.int32, (ROWS, 1), 0)
    offset = (row // 16) * 64 + quarter * 16 + row % 16
    spots = lax.broadcasted_iota(jnp.int32, (ROWS, KEYS), 1)
    zero = jnp.zeros((ROWS, 128), F32)

    def start_of(position):
        return jnp.where(position >= third, third, jnp.where(position >= second, second, 0))

    def work(tile, fixed):
        if fixed:
            rows = slice(tile * ROWS, (tile + 1) * ROWS)
        else:
            rows = pl.ds(mult(tile * ROWS, ROWS), ROWS)
        base = tile * KEYS
        both = q_grad[rows, :]
        position = base + offset
        query = jnp.where(left, both, jnp.zeros_like(both))

        def cut_of(j):
            if fixed:
                return slice(j * KEYS, (j + 1) * KEYS)
            return pl.ds(mult(j * KEYS, KEYS), KEYS)

        def loop(first, last, body, state):
            if fixed:
                for j in range(first, last):
                    state = body(j, state)
                return state
            return lax.fori_loop(first, last, body, state)

        def fold(top, part):
            for c in range(KEYS // 128):
                top = jnp.maximum(top, part[:, c * 128 : c * 128 + 128])
            return top

        def plain(j, top):
            part = mm(query, kv[cut_of(j), :], NT)
            scores[:, cut_of(j)] = part
            return fold(top, part)

        if fixed:
            low, high = 0, 0
        else:
            start = start_of(position)
            low = jnp.minimum(start_of(base + quarter * 16) // KEYS, tile)
            high = (start_of(base + KEYS - 64 + quarter * 16 + 15) + KEYS - 1) // KEYS
            high = jnp.minimum(jnp.maximum(high, low), tile)

        def masked(j, top):
            part = mm(query, kv[cut_of(j), :], NT)
            key_at = spots + j * KEYS
            allowed = key_at <= position
            if not fixed:
                allowed &= key_at >= start
            part = jnp.where(allowed, part, NEG_FILL)
            scores[:, cut_of(j)] = part
            return fold(top, part)

        top = jnp.full((ROWS, 128), NEG_FILL, F32)
        top = loop(low, high, masked, top)
        top = loop(high, tile, plain, top)
        top = masked(tile, top)
        row_top = jnp.max(top, axis=1, keepdims=True)

        def weigh(j, state):
            total, mixed = state
            part = jnp.exp(scores[:, cut_of(j)] - row_top)
            for c in range(KEYS // 128):
                total = total + part[:, c * 128 : c * 128 + 128]
            rounded = part.astype(BF)
            chances[:, cut_of(j)] = rounded
            return total, mixed + mm(rounded, kv[cut_of(j), :])

        total, mixed = loop(low, tile + 1, weigh, (zero, zero))
        share = 1.0 / jnp.sum(total, axis=1, keepdims=True)
        mixed = mixed * share
        scaled = jnp.where(left, both.astype(F32), both.astype(F32) * share)
        grad = jnp.where(left, 0.0, scaled)
        delta = jnp.sum(grad * mixed, axis=1, keepdims=True)
        grad = grad.astype(BF)
        turned = scaled.T.astype(BF)
        query_turned, grad_turned = turned[:64], turned[64:]

        def back(j, query_sum):
            cut = cut_of(j)
            part = chances[:, cut]
            along = mm(grad, kv[cut, :], NT)
            score_grad = (part.astype(F32) * (along - delta)).astype(BF)
            key_sums[0:64, cut] += mm(query_turned, score_grad)
            key_sums[64:128, cut] += mm(grad_turned, part)
            return query_sum + mm(score_grad, kv[cut, :])

        query_sum = loop(low, tile + 1, back, zero)
        rows_out[rows, :] = jnp.where(left, query_sum * 0.125, mixed).astype(BF)

    for tile in range(4):
        work(tile, True)

    @pl.loop(0, 4)
    def _(step):
        work(7 - step, False)

    @pl.loop(0, 8)
    def _(c):
        for d in range(8):
            cut = pl.ds(mult(c * 1024 + d * 128, 128), 128)
            kv[cut, :] = key_sums[:, cut].T.astype(BF)

    def spill(target, to_core):
        @pl.loop(0, 8)
        def _(step):
            for unrolled in range(4):
                i = step * 4 + unrolled
                group, half_x = i // 2, i % 2
                block = block_map[i * 2 + to_core]
                mirror = 127 - block
                target[group, pl.ds(mult(half_x * 128, 64), 64), :] = kv[
                    pl.ds(mult(block * 64, 64), 64), :
                ]
                target[group, pl.ds(mult(half_x * 128 + 64, 64), 64), :] = kv[
                    pl.ds(mult(mirror * 64, 64), 64), :
                ]
                spot = 256 + half_x * 32
                target[group, pl.ds(mult(spot, 16), 16), :] = rows_out[
                    pl.ds(mult(block * 16, 16), 16), :
                ]
                target[group, pl.ds(mult(spot + 16, 16), 16), :] = rows_out[
                    pl.ds(mult(mirror * 16, 16), 16), :
                ]

    spill(out_own, core)
    spill(out_other, 1 - core)


def return_kernel(
    place, back, cosine, sine, normed, xhat, upstream, weight, weight_mine,
    weight_other, early, out_own, out_other, normed_grad, project_grad, mixed_out, heads, small,
    weight_here, sems,
):
    core, chip = place[0], place[1]
    here, mine, others = halves(place[2], core)
    copies = fetch(qkv_copies(weight, chip, weight_here, sems))
    left = lax.broadcasted_iota(jnp.int32, (128, 128), 1) < 64
    for behind in range(4):
        origin = (chip + 4 - behind) % 4
        stream, half_x = origin // 2, origin % 2
        rows = pl.ds(behind * 128, 128)
        cos = cosine[rows, :]
        low, high = sine_parts(sine[rows, :], -1.0)
        for pair in range(2):
            pieces = []
            for member in range(2):
                base = stream * 8 + (pair * 2 + member) * 2
                cut = pl.ds(mult(half_x * 128, 128), 128)
                key_value = back[base, cut, :].astype(F32) + back[base + 1, cut, :].astype(F32)
                for upper in range(2):
                    for half in range(2):
                        for of_core in range(2):
                            flipped = of_core ^ core
                            spot = 256 + flipped * 64 + (half_x * 2 + upper) * 16
                            heads[
                                member, pl.ds(upper * 64 + (half * 2 + of_core) * 16, 16), :
                            ] = back[base + half, pl.ds(mult(spot, 16), 16), :]
                pieces.append((heads[member].astype(F32), key_value))
            (row0, kv0), (row1, kv1) = pieces
            at = pair * 128
            query = jnp.where(left, row0, pltpu.roll(row1, 64, 1))
            key = jnp.where(left, kv0, pltpu.roll(kv1, 64, 1))
            value = jnp.where(left, pltpu.roll(kv0, 64, 1), kv1)
            mixed = jnp.where(left, pltpu.roll(row0, 64, 1), row1)
            project_grad[rows, at : at + 128] = turn(query, cos, low, high).astype(BF)
            project_grad[rows, 256 + at : 384 + at] = turn(key, cos, low, high).astype(BF)
            project_grad[rows, 512 + at : 640 + at] = value.astype(BF)
            mixed_out[rows, at : at + 128] = mixed.astype(BF)

    small[...] = jnp.zeros_like(small)
    for k in range(32):
        small[0, k // 2, k % 2 : k % 2 + 1, :] = early[k : k + 1, :]

    def keep(first, sums):
        for n in range(sums.shape[1] // 128):
            k = first + n
            small[1, k // 2, k % 2 : k % 2 + 1, :] = sums[:, n * 128 : n * 128 + 128]

    for copy in copies:
        copy.wait()
    gain_sums = jnp.zeros((1, 1024), F32)
    shift_sums = jnp.zeros((1, 1024), F32)
    bias_sums = jnp.zeros((1, 768), F32)
    for block in range(4):
        rows = pl.ds(block * 128, 128)
        grads = project_grad[rows, :]
        normed_grad[rows, here] = mm(grads, weight_here[...], NT)
        normed_grad[rows, mine] = mm(grads, weight_mine[...], NT)
        normed_grad[rows, others] = mm(grads, weight_other[...], NT)
        entry = normed_grad[rows, :]
        gain_sums += jnp.sum(entry * xhat[rows, :].astype(F32), axis=0, keepdims=True)
        shift_sums += jnp.sum(entry, axis=0, keepdims=True)
        bias_sums += jnp.sum(grads.astype(F32), axis=0, keepdims=True)
    keep(0, gain_sums)
    keep(8, shift_sums)
    keep(16, bias_sums)

    for flip, target in ((0, out_own), (1, out_other)):
        to_core = core ^ flip
        for part in range(2):
            columns = normed[:, pl.ds(mult(part * 512 + to_core * 256, 256), 256)]
            for block in range(3):
                grads = mm(columns, project_grad[:, block * 256 : block * 256 + 256], TN).astype(BF)
                for n in range(2):
                    slot = part * 6 + block * 2 + n
                    target[:, slot * 16 : slot * 16 + 16, :] = grads[:, n * 128 : n * 128 + 128].reshape(
                        16, 16, 128
                    )
        for block in range(2):
            columns = upstream[:, pl.ds(mult(to_core * 512 + block * 256, 256), 256)]
            grads = mm(mixed_out[...], columns, TN).astype(BF)
            for n in range(2):
                at = 192 + (block * 2 + n) * 16
                target[:, at : at + 16, :] = grads[:, n * 128 : n * 128 + 128].reshape(16, 16, 128)
        target[:, 256:272, :] = small[to_core].astype(BF)


def feed_kernel(
    place, gains, vector, normed, upstream, xhat, weight, weight_mine, weight_other, proj,
    out_own, out_other, branch, entry, early, active, inner_grad, sums, weight_here, proj_here, sems,
):
    core, chip, half_in, low_x = place[0], place[1], place[2], place[3]
    here, mine, others = halves(half_in, core)
    copies = fetch(
        [
            (weight.at[:, pl.ds(mult(chip * 1024, 1024), 1024)], weight_here, sems.at[0]),
            (proj.at[pl.ds(mult(low_x * 1024, 1024), 1024), :], proj_here, sems.at[1]),
        ]
    )
    bias = jnp.concatenate([vector[pl.ds(7 + low_x * 2, 1), :], vector[pl.ds(8 + low_x * 2, 1), :]], axis=1)
    sums[...] = jnp.zeros_like(sums)
    sums[2:3, :] = jnp.sum(upstream[0:128, :].astype(F32), axis=0, keepdims=True)
    copies[0].wait()
    for block in range(2):
        rows = pl.ds(block * 256, 256)
        inner = (
            mm(normed[rows, here], weight_here[...])
            + mm(normed[rows, mine], weight_mine[...])
            + mm(normed[rows, others], weight_other[...])
            + bias
        )
        bell = 0.5 * (1.0 + lax.erf(inner * (2.0**-0.5)))
        act = (inner * bell).astype(BF)
        active[rows, :] = act
        if block == 0:
            copies[1].wait()
        branch[rows, :] = mm(act, proj_here[...])
        slope = bell + inner * jnp.exp(-0.5 * inner * inner) * (1.0 / math.sqrt(2.0 * math.pi))
        grad = (mm(upstream[rows, :], proj_here[...], NT) * slope).astype(BF)
        inner_grad[rows, :] = grad
        sums[3:4, :] += jnp.sum(grad.astype(F32), axis=0, keepdims=True)
        for cut, part in ((here, weight_here), (mine, weight_mine), (others, weight_other)):
            back = mm(grad, part[...], NT)
            entry[rows, cut] = back * gains[2:3, cut]
            sums[0:1, cut] += jnp.sum(back * xhat[rows, cut].astype(F32), axis=0, keepdims=True)
            sums[1:2, cut] += jnp.sum(back, axis=0, keepdims=True)
    for k in range(32):
        at = (k % 8) * 128
        early[k : k + 1, :] = sums[k // 8 : k // 8 + 1, at : at + 128]

    for flip, target in ((0, out_own), (1, out_other)):
        to_core = core ^ flip
        for part in range(2):
            features = normed[:, pl.ds(mult(part * 512 + to_core * 256, 256), 256)]
            for quad in range(4):
                grads = mm(features, inner_grad[:, quad * 256 : quad * 256 + 256], TN).astype(BF)
                for n in range(2):
                    slot = part * 8 + quad * 2 + n
                    target[:, slot * 16 : slot * 16 + 16, :] = grads[:, n * 128 : n * 128 + 128].reshape(
                        16, 16, 128
                    )
        features = active[:, pl.ds(mult(to_core * 512, 512), 512)]
        for quad in range(4):
            grads = mm(features, upstream[:, quad * 256 : quad * 256 + 256], TN).astype(BF)
            for n in range(2):
                at = 256 + (quad * 2 + n) * 32
                target[:, at : at + 32, :] = grads[:, n * 128 : n * 128 + 128].reshape(16, 32, 128)


def combine_kernel(own, arrived, out):
    out[:, 0:256, :] = (own[:, 0:256, :].astype(F32) + arrived[:, 0:256, :].astype(F32)).astype(BF)
    out[:, 256:320, :] = own[:, 256:320, :]
    out[:, 320:384, :] = arrived[:, 256:320, :]


def rows_kernel(place, branch, mixed, out_weight, normed_grad, entry, gains, *outs):
    weight = out_weight[pl.ds(mult(place[3] * 256, 256), 256), :]
    for block, out in enumerate(outs):
        rows = pl.ds(block * 128, 128)
        out[0:128, :] = (branch[rows, :] + mm(mixed[rows, :], weight)).astype(BF)
        out[128:256, :] = (normed_grad[rows, :] * gains[0:1, :] + entry[rows, :]).astype(BF)


def finish_kernel(hidden, upstream, rows0, rows1, rows2, rows3, bias, hidden_out, hidden_grad):
    shares = [part.astype(F32) for part in (rows0[...], rows1[...], rows2[...], rows3[...])]
    total = (shares[0] + shares[1]) + (shares[2] + shares[3])
    full = hidden[...].astype(F32)
    hidden_out[...] = (full + total[:128] + bias[...]).astype(BF)
    xhat, scale = normalized(full)
    entry = total[128:]
    hidden_grad[...] = upstream[...].astype(F32) + scale * (
        entry
        - jnp.mean(entry, axis=1, keepdims=True)
        - xhat * jnp.mean(entry * xhat, axis=1, keepdims=True)
    )


def spread_kernel(place, piece, out, *, columns):
    for behind, slot, rows, step, at in columns:
        start = at
        if step:
            start = mult(at + ((place[1] + 4 - behind) % 4) * step, 128)
        part = piece[:, slot : slot + rows, :].astype(F32)
        out[:, pl.ds(start, 128)] = part.reshape(piece.shape[0] * rows, 128)


def spread(place, pieces, at_rows, shape_out, block, grid, in_map, out_map, columns):
    return pl.pallas_call(
        functools.partial(spread_kernel, columns=columns),
        out_shape=jax.ShapeDtypeStruct(shape_out, F32),
        grid_spec=pltpu.PrefetchScalarGridSpec(
            num_scalar_prefetch=1,
            grid=grid,
            in_specs=[pl.BlockSpec((8, at_rows, 128), in_map)],
            out_specs=pl.BlockSpec(block, out_map),
        ),
        compiler_params=pltpu.CompilerParams(vmem_limit_bytes=60 * MIB),
    )(place, pieces)


def heads_spread_kernel(place, piece, *refs):
    qkv, out = refs[-2:]
    for behind in range(4):
        start = ((place[1] + 4 - behind) % 4) * 256
        for n in range(6):
            slot = behind * 112 + n * 16
            at = mult((n // 2) * 1024 + (n % 2) * 128 + start, 128)
            qkv[:, pl.ds(at, 128)] = piece[:, slot : slot + 16, :].astype(F32).reshape(128, 128)
    for flip in range(2):
        for n in range(4):
            slot = 448 + flip * 64 + n * 16
            out[place[3] ^ flip, :, n * 128 : n * 128 + 128] = (
                piece[:, slot : slot + 16, :].astype(F32).reshape(128, 128)
            )


def heads_spread(place, pieces, flip, before=()):
    return pl.pallas_call(
        heads_spread_kernel,
        out_shape=[shape(512, 3072, dtype=F32), shape(2, 256, 1024, dtype=F32)],
        grid_spec=pltpu.PrefetchScalarGridSpec(
            num_scalar_prefetch=1,
            grid=(2,),
            in_specs=[pl.BlockSpec((8, 576, 128), lambda g, place: (g, 0, 0))]
            + [pl.BlockSpec(memory_space=pl.ANY) for _ in before],
            out_specs=[
                pl.BlockSpec((128, 3072), lambda g, place: ((place[0] ^ flip) * 2 + g, 0)),
                pl.BlockSpec((2, 128, 512), lambda g, place: (0, g, place[0] ^ flip)),
            ],
        ),
        input_output_aliases={2 + k: k for k in range(len(before))},
        compiler_params=pltpu.CompilerParams(vmem_limit_bytes=60 * MIB),
    )(place, pieces, *before)


def shape(*sizes, dtype=BF):
    return jax.ShapeDtypeStruct(sizes, dtype)


def normalized(hidden):
    moved = hidden - jnp.mean(hidden, axis=-1, keepdims=True)
    spread_out = jnp.mean(moved * moved, axis=-1, keepdims=True)
    scale = lax.rsqrt(spread_out + EPS)
    return moved * scale, scale


def per_device(
    hidden_in, doc_ids, block_map, attn_gain, attn_shift, mlp_gain, mlp_shift, qkv_weight, qkv_bias,
    out_weight, out_bias, in_weight, in_bias, proj_weight, proj_bias, cotangent,
):
    y, z = lax.axis_index("y"), lax.axis_index("z")
    xh, xl = lax.axis_index("xh"), lax.axis_index("xl")
    core = lax.axis_index("core")
    group = y * 4 + z
    chip = xh * 2 + xl
    low_half = xh == 0
    smem = whole(pltpu.SMEM)
    place = jnp.stack([core, chip, xh, xl, group]).astype(jnp.int32)

    partner = (1 - xh) * 2 + xl
    piece = jnp.concatenate(
        [
            lax.dynamic_slice(qkv_weight, (core * 256, k * 1024 + partner * 256), (256, 256))
            for k in range(3)
        ],
        axis=1,
    )
    payload = jnp.stack([hidden_in[0], cotangent[0]])
    piece, payload = lax.optimization_barrier((piece, payload))
    qkv_mine = swap(piece, "xh")
    qkv_other = swap(qkv_mine, "core")
    ring = [payload] + [shift_ring(payload, d) for d in (1, 2, 3)]
    parts = (attn_gain, attn_shift, mlp_gain, mlp_shift, qkv_bias, in_bias, out_bias, proj_bias)
    (vector,) = call(vector_kernel, [shape(16, 512, dtype=F32)], [whole()] * 9)(
        *[part.reshape(1, -1) for part in parts], doc_ids.reshape(64, 128)
    )
    vector_other = swap(vector, "xh")

    in_weight_late, qkv_mine, vector = lax.optimization_barrier((in_weight, qkv_mine, vector))
    in_mine = swap(lax.dynamic_slice(in_weight_late, (core * 256, partner * 1024), (256, 1024)), "xh")
    in_other = swap(in_mine, "core")

    frequency = 10000.0 ** (-(jnp.arange(0, ROT, 2).astype(F32) / ROT))
    lanes = jnp.concatenate([frequency, frequency, jnp.zeros((48,), F32)])
    lanes = jnp.concatenate([lanes, lanes])[None]
    send, normed, normed_mlp, xhat, upstream, cosine, sine, gains = call(
        project_kernel,
        [shape(16, 384, 128)]
        + [shape(512, 1024)] * 4
        + [shape(512, 128, dtype=F32)] * 2
        + [shape(4, 1024, dtype=F32)],
        [smem] * 2 + [whole()] * 7 + [whole(pl.ANY)] + [whole()] * 2 + [whole(pl.ANY)],
        scratch=[
            pltpu.VMEM((512, 768), BF),
            pltpu.VMEM((256, 1024), BF),
            pltpu.SemaphoreType.DMA((4,)),
        ],
    )(place, block_map, *ring, vector, vector_other, lanes, qkv_weight, qkv_mine, qkv_other, out_weight)
    heads_own = lax.all_to_all(send, PLANE, 0, 0, tiled=True)

    feed_own, feed_other, branch, entry, early = call(
        feed_kernel,
        [shape(16, 512, 128)] * 2 + [shape(512, 1024, dtype=F32)] * 2 + [shape(32, 128, dtype=F32)],
        [smem] + [whole()] * 5 + [whole(pl.ANY)] + [whole()] * 2 + [whole(pl.ANY)],
        scratch=[pltpu.VMEM((512, 1024), BF)] * 2
        + [
            pltpu.VMEM((4, 1024), F32),
            pltpu.VMEM((512, 1024), BF),
            pltpu.VMEM((1024, 1024), BF),
            pltpu.SemaphoreType.DMA((2,)),
        ],
    )(place, gains, vector, normed_mlp, upstream, xhat, in_weight, in_mine, in_other, proj_weight)
    feed_both = feed_own + swap(feed_other, "core")

    def reduce_plane(both):
        parts = lax.all_to_all(both, PLANE, 0, 0, tiled=True)
        return jnp.sum(parts.astype(F32), axis=0)

    def around(parts, rest=()):
        got = [jnp.concatenate([lax.dynamic_index_in_dim(parts, xh, 0, False), *rest])]
        for d in (1, 2, 3):
            half = ((chip + d) % 4) // 2
            got.append(
                shift_ring(jnp.concatenate([lax.dynamic_index_in_dim(parts, half, 0, False), *rest]), d)
            )
        return got

    heads_other = swap(heads_own, "core")
    heads_own, heads_other, feed_both, early, entry, branch = lax.optimization_barrier(
        (heads_own, heads_other, feed_both, early, entry, branch)
    )
    feed = reduce_plane(feed_both)
    quarter = (group % 2) * 2 + core
    bounds = jnp.where(group // 8 == xh, vector[13, :2], vector_other[13, :2])
    spot = jnp.concatenate([jnp.stack([core, quarter]).astype(jnp.int32), bounds.astype(jnp.int32)])
    back_own, back_other = call(
        attend_kernel,
        [shape(16, 320, 128)] * 2,
        [smem, smem] + [whole()] * 2,
        scratch=[
            pltpu.VMEM((8192, 128), BF),
            pltpu.VMEM((2048, 128), BF),
            pltpu.VMEM((ROWS, 8192), F32),
            pltpu.VMEM((ROWS, 8192), BF),
            pltpu.VMEM((128, 8192), F32),
            pltpu.VMEM((2048, 128), BF),
        ],
        flops=45 * 10**9,
        moved=6 * MIB,
    )(spot, block_map, heads_own, heads_other)

    (returning,) = call(combine_kernel, [shape(16, 384, 128)], [whole()] * 2)(
        back_own, swap(back_other, "core")
    )
    feed = feed.astype(BF)
    in_parts = around(feed[:256].reshape(2, 128, 128))
    proj_parts = [feed[256:], swap(feed[256:], "xl")]
    feed_parts = jnp.concatenate(in_parts + proj_parts)
    feed_parts, returning = lax.optimization_barrier((feed_parts, returning))
    feed_all = lax.all_gather(feed_parts, ("core",) + PLANE, axis=0)
    returned = lax.all_to_all(returning, PLANE, 0, 0, tiled=True)
    heads_grad_own, heads_grad_other, normed_grad, project_grad, mixed = call(
        return_kernel,
        [shape(16, 272, 128)] * 2 + [shape(512, 1024, dtype=F32), shape(512, 768), shape(512, 256)],
        [smem] + [whole()] * 6 + [whole(pl.ANY)] + [whole()] * 3,
        scratch=[
            pltpu.VMEM((2, 128, 128), BF),
            pltpu.VMEM((2, 16, 16, 128), F32),
            pltpu.VMEM((512, 768), BF),
            pltpu.SemaphoreType.DMA((3,)),
        ],
    )(place, returned, cosine, sine, normed, xhat, upstream, qkv_weight, qkv_mine, qkv_other, early)
    heads_both = heads_grad_own + swap(heads_grad_other, "core")
    heads_sum = reduce_plane(heads_both).astype(BF)

    to_rows = call(rows_kernel, [shape(256, 1024)] * 4, [smem] + [whole()] * 6)(
        place, branch, mixed, out_weight, normed_grad, entry, gains
    )
    heads_sum, *to_rows = lax.optimization_barrier((heads_sum, *to_rows))

    heads_parts = around(heads_sum[:192].reshape(2, 96, 128), (heads_sum[256:], heads_sum[192:256]))
    beside = jnp.where(xl == 0, heads_parts[3], heads_parts[1])
    gathering = jnp.concatenate(
        [part[:112] for part in heads_parts] + [heads_parts[0][112:], beside[112:]]
    )
    gathering, *to_rows = lax.optimization_barrier((gathering, *to_rows))
    heads_all = to_all(gathering, PLANE, 16)

    arrived = [to_rows[0]] + [shift_ring(to_rows[d], 4 - d) for d in (1, 2, 3)]
    bias_here, bias_there = [part[11] + part[12] for part in (vector, vector_other)]
    in_weight_grad = spread(
        place, feed_all, 512, (512, 4096), (128, 4096), (4,),
        lambda g, place: (g, 0, 0), lambda g, place: (g, 0),
        [(c, c * 128 + n * 16, 16, 1024, n * 128) for c in range(4) for n in range(8)],
    )
    proj_weight_grad = spread(
        place, feed_all, 256, (2048, 1024), (256, 1024), (2, 4),
        lambda a, g, place: (g, 2 + a, 0), lambda a, g, place: ((place[3] ^ a) * 4 + g, 0),
        [(0, n * 32, 32, 0, n * 128) for n in range(8)],
    )
    heads_all, in_weight_grad, proj_weight_grad, *arrived = lax.optimization_barrier(
        (heads_all, in_weight_grad, proj_weight_grad, *arrived)
    )
    heads_core = swap(heads_all, "core")
    hidden_out, hidden_grad = call(
        finish_kernel, [shape(128, 1024), shape(128, 1024, dtype=F32)], [whole()] * 7
    )(hidden_in[0], cotangent[0], *arrived, in_order(low_half, bias_here, bias_there).reshape(1, 1024))
    hidden_out, hidden_grad = hidden_out[None], hidden_grad[None]

    small = heads_all[:, :448].reshape(16, 4, 112, 128)[:, :, 96:98].reshape(16, 4, 256)
    small = in_order(core == 0, small, swap(small, "core")).astype(F32)
    small = small.transpose(2, 0, 1, 3).reshape(4, 2, 4, 1024)
    common = jnp.sum(small, axis=0)
    origins = (chip + 4 - jnp.arange(4, dtype=jnp.int32)) % 4
    in_order_of_chips = jnp.take(small, origins, axis=0)
    own_columns = lax.dynamic_slice(common, (0, 0, xh * 512), (2, 4, 512))
    in_bias_grad = lax.dynamic_slice(in_order_of_chips[:, 0, 3].reshape(4096), (xh * 2048,), (2048,))
    qkv_bias_grad = in_order_of_chips[:, 1, 2:].reshape(4, 2048)[:, :768].reshape(4, 3, 256)
    qkv_bias_grad = qkv_bias_grad.transpose(1, 0, 2).reshape(3072)
    qkv_bias_grad = lax.dynamic_slice(qkv_bias_grad, (xh * 1536,), (1536,))

    partial = heads_spread(place, heads_all, 0)
    qkv_weight_grad, out_weight_grad = heads_spread(place, heads_core, 1, partial)
    out_weight_grad = out_weight_grad.reshape(512, 1024)

    return (
        hidden_out, hidden_grad, own_columns[1, 0], own_columns[1, 1], own_columns[0, 0],
        own_columns[0, 1], qkv_weight_grad, qkv_bias_grad, out_weight_grad, own_columns[0, 2],
        in_weight_grad, in_bias_grad, proj_weight_grad, own_columns[0, 2],
    )


def solution(mesh):
    fine = Mesh(mesh.devices.reshape(4, 4, 2, 2, 2), ("y", "z", "xl", "core", "xh"))
    ctx = ("y", "z", "xl", "core")
    rows = P("xh", ctx, None)
    half = P("xh")
    wide = P("xh", None)
    in_specs = (
        rows, wide, P(), half, half, half, half, wide, half, wide, half, wide, half, wide, half, rows,
    )
    out_specs = (
        rows, rows, half, half, half, half, wide, half, wide, half, wide, half, wide, half,
    )
    return jax.shard_map(
        per_device, mesh=fine, in_specs=in_specs, out_specs=out_specs, check_vma=False
    )
```

```python
import functools
import math

import jax
import jax.numpy as jnp
from jax import lax
from jax.experimental import pallas as pl
from jax.experimental.pallas import tpu as pltpu
from jax.sharding import Mesh
from jax.sharding import PartitionSpec as P

ROT = 16
EPS = 1e-05
NEG_FILL = -1e30
BF = jnp.bfloat16
F32 = jnp.float32
RING = ("xh", "xl")
PLANE = ("y", "z")
MIB = 1 << 20

NN = (((1,), (0,)), ((), ()))
NT = (((1,), (1,)), ((), ()))
TN = (((0,), (0,)), ((), ()))


def mm(left, right, dims=NN):
    return lax.dot_general(left, right, dims, preferred_element_type=F32)


def mult(value, step):
    return pl.multiple_of(value, step)


def whole(space=pltpu.VMEM):
    return pl.BlockSpec(memory_space=space)


def call(body, outs, ins, scratch=(), flops=0, moved=0, limit=60, grid=()):
    return pl.pallas_call(
        body,
        out_shape=outs,
        grid=grid,
        in_specs=ins,
        out_specs=[whole() for _ in outs],
        scratch_shapes=list(scratch),
        cost_estimate=pl.CostEstimate(flops=flops, bytes_accessed=moved, transcendentals=0),
        compiler_params=pltpu.CompilerParams(vmem_limit_bytes=limit * MIB),
    )


def held(*arrays):
    return pl.pallas_call(
        lambda *refs: None,
        out_shape=[jax.ShapeDtypeStruct(a.shape, a.dtype) for a in arrays],
        in_specs=[whole(pl.ANY) for _ in arrays],
        out_specs=[whole(pl.ANY) for _ in arrays],
        input_output_aliases={k: k for k in range(len(arrays))},
        cost_estimate=pl.CostEstimate(flops=2 * 10**9, bytes_accessed=0, transcendentals=0),
    )(*arrays)


def to_all(array_in, axes, count):
    copies = jnp.broadcast_to(array_in[None], (count,) + array_in.shape)
    return lax.all_to_all(copies, axes, 0, 0, tiled=True)


def swap(array_in, axis):
    return lax.ppermute(array_in, axis, [(0, 1), (1, 0)])


def shift_ring(array_in, places):
    spots = [(x % 2) * 2 + x // 2 for x in range(4)]
    return lax.ppermute(
        array_in, ("xl", "xh"), [(spots[x], spots[(x + places) % 4]) for x in range(4)]
    )


def cross(array_in):
    return lax.ppermute(array_in, ("xl", "xh"), [(0, 3), (1, 2), (2, 1), (3, 0)])


def in_order(first, mine, other):
    return jnp.where(first, jnp.stack([mine, other]), jnp.stack([other, mine]))


def turn(tile, cosine, sine_low, sine_high):
    return (
        tile * cosine
        + pltpu.roll(tile, 120, 1) * sine_low
        + pltpu.roll(tile, 8, 1) * sine_high
    )


def sine_parts(sine, sign):
    spot = lax.broadcasted_iota(jnp.int32, sine.shape, 1) % 64
    low = jnp.where(spot < 8, -sign * sine, 0.0)
    high = jnp.where((spot >= 8) & (spot < 16), sign * sine, 0.0)
    return low, high


def wide_row(vector, first, count):
    return jnp.concatenate([vector[first + k : first + k + 1, :] for k in range(count)], axis=1)


def halves(half_in, core):
    start = 512 - half_in * 512
    return (
        pl.ds(mult(half_in * 512, 512), 512),
        pl.ds(mult(start + core * 256, 256), 256),
        pl.ds(mult(start + 256 - core * 256, 256), 256),
    )


def fetch(copies):
    started = [pltpu.make_async_copy(*copy) for copy in copies]
    for copy in started:
        copy.start()
    return started


def qkv_copies(weight, chip, target, sems):
    return [
        (
            weight.at[:, pl.ds(mult(k * 1024 + chip * 256, 256), 256)],
            target.at[:, pl.ds(k * 256, 256)],
            sems.at[k],
        )
        for k in range(3)
    ]


def project_kernel(
    place, block_map, rows0, rows1, rows2, rows3, vector, vector_other, lanes, weight, weight_mine,
    weight_other, out_weight, send, normed, normed_mlp, xhat, upstream, cosine, sine, gains,
    weight_here, out_here, sems,
):
    own_core, chip, half_in, low_x, group = place[0], place[1], place[2], place[3], place[4]
    here, mine, others = halves(half_in, own_core)
    copies = fetch(
        qkv_copies(weight, chip, weight_here, sems)
        + [(out_weight.at[pl.ds(mult(low_x * 256, 256), 256), :], out_here, sems.at[3])]
    )
    there = pl.ds(mult(512 - half_in * 512, 512), 512)
    for k in range(4):
        gains[k : k + 1, here] = wide_row(vector, k * 4, 4)
        gains[k : k + 1, there] = wide_row(vector_other, k * 4, 4)
    left = lax.broadcasted_iota(jnp.int32, (64, 128), 1) < 64
    left_all = lax.broadcasted_iota(jnp.int32, (128, 128), 1) < 64
    row = lax.broadcasted_iota(jnp.int32, (128, 1), 0)

    def pack(tile):
        low, high = tile[:64], tile[64:]
        return (
            jnp.where(left, low, pltpu.roll(high, 64, 1)).astype(BF),
            jnp.where(left, pltpu.roll(low, 64, 1), high).astype(BF),
        )

    def bias_of(k):
        at = k * 1024 + chip * 256
        spot = 16 + (at % 1536) // 128
        parts = [
            jnp.where(at // 1536 == half_in, vector[pl.ds(spot + n, 1), :], vector_other[pl.ds(spot + n, 1), :])
            for n in range(2)
        ]
        return jnp.concatenate(parts, axis=1)

    biases = [bias_of(k) for k in range(3)]
    for copy in copies:
        copy.wait()
    for back, source in enumerate((rows0, rows1, rows2, rows3)):
        origin = (chip + 4 - back) % 4
        stream, half_x = origin // 2, origin % 2
        rows = pl.ds(back * 128, 128)
        moved = source[0].astype(F32)
        moved = moved - jnp.mean(moved, axis=1, keepdims=True)
        spread = jnp.mean(moved * moved, axis=1, keepdims=True)
        unit = moved * lax.rsqrt(spread + EPS)
        xhat[rows, :] = unit.astype(BF)
        normed[rows, :] = (unit * gains[0:1, :] + gains[1:2, :]).astype(BF)
        normed_mlp[rows, :] = (unit * gains[2:3, :] + gains[3:4, :]).astype(BF)
        upstream[rows, :] = source[1]

        block = block_map[(group * 2 + half_x) * 2 + own_core]
        position = jnp.where(row < 64, block * 64 + row, (127 - block) * 64 + row - 64).astype(F32)
        same = stream == half_in
        second = jnp.where(same, vector[52:53, 0:1], vector_other[52:53, 0:1])
        third = jnp.where(same, vector[52:53, 1:2], vector_other[52:53, 1:2])
        first = jnp.where(position >= third, third, jnp.where(position >= second, second, 0.0))
        angles = (position - first) * lanes[...]
        cos, sin = jnp.cos(angles), jnp.sin(angles)
        cosine[rows, :] = cos
        sine[rows, :] = sin
        low, high = sine_parts(sin, 1.0)

        def project(k):
            columns = slice(k * 256, k * 256 + 256)
            return (
                mm(normed[rows, here], weight_here[:, columns])
                + mm(normed[rows, mine], weight_mine[:, columns])
                + mm(normed[rows, others], weight_other[:, columns])
                + biases[k]
            )

        queries, keys, values = project(0), project(1), project(2)
        grads = mm(source[1], out_here[...], NT)
        for pair in range(2):
            at = pair * 128
            query = pack(turn(queries[:, at : at + 128], cos, low, high) * 0.125)
            grad = pack(grads[:, at : at + 128])
            key = turn(keys[:, at : at + 128], cos, low, high)
            value = values[:, at : at + 128]
            key_value = (
                jnp.where(left_all, key, pltpu.roll(value, 64, 1)).astype(BF),
                jnp.where(left_all, pltpu.roll(key, 64, 1), value).astype(BF),
            )
            for member in range(2):
                for half in range(2):
                    target = stream * 8 + (pair * 2 + member) * 2 + half
                    send[target, pl.ds(mult(half_x * 128, 128), 128), :] = key_value[member]
                    for core in range(2):
                        quarter = half * 2 + core
                        cut = slice(quarter * 16, quarter * 16 + 16)
                        spot = core * 32 + half_x * 16
                        send[target, pl.ds(mult(256 + spot, 16), 16), :] = query[member][cut]
                        send[target, pl.ds(mult(320 + spot, 16), 16), :] = grad[member][cut]


ROWS = 256
KEYS = 1024
STRAIGHT = (2, 3, 4, 5)


def attend_scratch():
    return [
        pltpu.VMEM((8192, 128), BF),
        pltpu.VMEM((2048, 128), BF),
        pltpu.VMEM((ROWS, 8192), F32),
        pltpu.VMEM((ROWS, 8192), BF),
        pltpu.VMEM((128, 8192), F32),
        pltpu.VMEM((2048, 128), BF),
    ]


def attend_kernel(
    place, block_map, own, other, out_own, out_other, kv, q_grad, scores, chances, key_sums, rows_out,
):
    core, quarter, second, third = place[0], place[1], place[2], place[3]
    left16 = lax.broadcasted_iota(jnp.int32, (16, 128), 1) < 64
    left = lax.broadcasted_iota(jnp.int32, (ROWS, 128), 1) < 64

    def blocks_of(from_core, body):
        @pl.loop(0, 8)
        def _(step):
            for unrolled in range(4):
                i = step * 4 + unrolled
                block = block_map[i * 2 + from_core]
                body(i // 2, i % 2, block, 127 - block)

    def fill(source, from_core):
        def body(group, half_x, block, mirror):
            for upper, to in ((0, block), (1, mirror)):
                kv[pl.ds(mult(to * 64, 64), 64), :] = source[
                    group, pl.ds(mult(half_x * 128 + upper * 64, 64), 64), :
                ]
            spot = core * 32 + half_x * 16
            query = source[group, pl.ds(mult(256 + spot, 16), 16), :].astype(F32)
            grad = source[group, pl.ds(mult(320 + spot, 16), 16), :].astype(F32)
            q_grad[pl.ds(mult(block * 16, 16), 16), :] = jnp.where(
                left16, query, pltpu.roll(grad, 64, 1)
            ).astype(BF)
            q_grad[pl.ds(mult(mirror * 16, 16), 16), :] = jnp.where(
                left16, pltpu.roll(query, 64, 1), grad
            ).astype(BF)

        blocks_of(from_core, body)

    fill(own, core)
    fill(other, 1 - core)
    key_sums[...] = jnp.zeros_like(key_sums)

    row = lax.broadcasted_iota(jnp.int32, (ROWS, 1), 0)
    offset = (row // 16) * 64 + quarter * 16 + row % 16

    def start_of(position):
        return jnp.where(position >= third, third, jnp.where(position >= second, second, 0))

    def join(first_row, old, new):
        return new if first_row == 0 else jnp.concatenate([old[:first_row], new], axis=0)

    def work(tile):
        rows = pl.ds(mult(tile * ROWS, ROWS), ROWS)
        base = tile * KEYS
        both = q_grad[rows, :]
        position = base + offset
        start = start_of(position)
        query = jnp.where(left, both, jnp.zeros_like(both))

        def whole_cut(j, masked):
            return (j * KEYS, KEYS, 0, masked and "start")

        diagonal = [(base, KEYS // 2, 0, "causal"), (base + KEYS // 2, KEYS // 2, ROWS // 2, "causal")]

        def keys_of(cut):
            return pl.ds(mult(cut[0], KEYS // 2), cut[1])

        def score(cut, top):
            first_key, width, first_row, masked = cut
            part = mm(query[first_row:], kv[keys_of(cut), :], NT)
            if masked:
                spots = lax.broadcasted_iota(jnp.int32, part.shape, 1)
                allowed = spots >= start[first_row:] - first_key
                if masked == "causal":
                    allowed &= spots <= position[first_row:] - first_key
                part = jnp.where(allowed, part, NEG_FILL)
            scores[first_row:, keys_of(cut)] = part
            best = top[first_row:]
            for c in range(width // 128):
                best = jnp.maximum(best, part[:, c * 128 : c * 128 + 128])
            return join(first_row, top, best)

        def weigh(cut, row_top, total, mixed):
            _, width, first_row, _ = cut
            part = jnp.exp(scores[first_row:, keys_of(cut)] - row_top[first_row:])
            sums = total[first_row:]
            for c in range(width // 128):
                sums = sums + part[:, c * 128 : c * 128 + 128]
            rounded = part.astype(BF)
            chances[first_row:, keys_of(cut)] = rounded
            values = mixed[first_row:] + mm(rounded, kv[keys_of(cut), :])
            return join(first_row, total, sums), join(first_row, mixed, values)

        def back(cut, grad, delta, query_turned, grad_turned, query_sum):
            _, _, first_row, _ = cut
            keys = keys_of(cut)
            part = chances[first_row:, keys]
            along = mm(grad[first_row:], kv[keys, :], NT)
            score_grad = (part.astype(F32) * (along - delta[first_row:])).astype(BF)
            key_sums[0:64, keys] += mm(query_turned[:, first_row:], score_grad)
            key_sums[64:128, keys] += mm(grad_turned[:, first_row:], part)
            sums = query_sum[first_row:] + mm(score_grad, kv[keys, :])
            return join(first_row, query_sum, sums)

        def passes(first, last, middle, cuts):
            zero = jnp.zeros((ROWS, 128), F32)
            top = jnp.full((ROWS, 128), NEG_FILL, F32)
            if first is not None:
                top = lax.fori_loop(first, middle, lambda j, v: score(whole_cut(j, True), v), top)
                top = lax.fori_loop(middle, last, lambda j, v: score(whole_cut(j, False), v), top)
            for cut in cuts:
                top = score(cut, top)
            row_top = jnp.max(top, axis=1, keepdims=True)
            state = (zero, zero)
            if first is not None:
                state = lax.fori_loop(
                    first, last, lambda j, v: weigh(whole_cut(j, False), row_top, *v), state
                )
            for cut in cuts:
                state = weigh(cut, row_top, *state)
            total, mixed = state
            share = 1.0 / jnp.sum(total, axis=1, keepdims=True)
            mixed = mixed * share
            scaled = jnp.where(left, both.astype(F32), both.astype(F32) * share)
            grad = jnp.where(left, 0.0, scaled)
            delta = jnp.sum(grad * mixed, axis=1, keepdims=True)
            grad = grad.astype(BF)
            turned = scaled.T.astype(BF)
            fixed_part = (grad, delta, turned[:64], turned[64:])
            query_sum = zero
            if first is not None:
                query_sum = lax.fori_loop(
                    first, last, lambda j, v: back(whole_cut(j, False), *fixed_part, v), query_sum
                )
            for cut in cuts:
                query_sum = back(cut, *fixed_part, query_sum)
            rows_out[rows, :] = jnp.where(left, query_sum * 0.125, mixed).astype(BF)

        low = jnp.minimum(start_of(base + quarter * 16) // KEYS, tile)
        count = tile + 1 - low
        usual = (count >= STRAIGHT[0]) & (count <= STRAIGHT[-1])
        for n in STRAIGHT:

            @pl.when(count == n)
            def _(n=n):
                passes(None, None, None, [whole_cut(low + i, True) for i in range(n - 1)] + diagonal)

        @pl.when(jnp.logical_not(usual))
        def _():
            high = (start_of(base + KEYS - 64 + quarter * 16 + 15) + KEYS - 1) // KEYS
            passes(low, tile, jnp.minimum(jnp.maximum(high, low), tile), diagonal)

    pl.loop(0, 8)(work)

    @pl.loop(0, 8)
    def _(c):
        for d in range(8):
            cut = pl.ds(mult(c * 1024 + d * 128, 128), 128)
            kv[cut, :] = key_sums[:, cut].T.astype(BF)

    def spill(target, to_core):
        def body(group, half_x, block, mirror):
            spot = 256 + half_x * 32
            for upper, at in ((0, block), (1, mirror)):
                target[group, pl.ds(mult(half_x * 128 + upper * 64, 64), 64), :] = kv[
                    pl.ds(mult(at * 64, 64), 64), :
                ]
                target[group, pl.ds(mult(spot + upper * 16, 16), 16), :] = rows_out[
                    pl.ds(mult(at * 16, 16), 16), :
                ]

        blocks_of(to_core, body)

    spill(out_own, core)
    spill(out_other, 1 - core)


def return_kernel(
    place, back, cosine, sine, normed, xhat, upstream, weight, weight_mine,
    weight_other, early, out_own, out_other, normed_grad, project_grad, mixed_out, heads, small,
    weight_here, sems,
):
    core, chip = place[0], place[1]
    here, mine, others = halves(place[2], core)
    copies = fetch(qkv_copies(weight, chip, weight_here, sems))
    left = lax.broadcasted_iota(jnp.int32, (128, 128), 1) < 64
    for behind in range(4):
        origin = (chip + 4 - behind) % 4
        stream, half_x = origin // 2, origin % 2
        rows = pl.ds(behind * 128, 128)
        cos = cosine[rows, :]
        low, high = sine_parts(sine[rows, :], -1.0)
        for pair in range(2):
            pieces = []
            for member in range(2):
                base = stream * 8 + (pair * 2 + member) * 2
                cut = pl.ds(mult(half_x * 128, 128), 128)
                key_value = back[base, cut, :].astype(F32) + back[base + 1, cut, :].astype(F32)
                for upper in range(2):
                    for half in range(2):
                        for of_core in range(2):
                            flipped = of_core ^ core
                            spot = 256 + flipped * 64 + (half_x * 2 + upper) * 16
                            heads[
                                member, pl.ds(upper * 64 + (half * 2 + of_core) * 16, 16), :
                            ] = back[base + half, pl.ds(mult(spot, 16), 16), :]
                pieces.append((heads[member].astype(F32), key_value))
            (row0, kv0), (row1, kv1) = pieces
            at = pair * 128
            query = jnp.where(left, row0, pltpu.roll(row1, 64, 1))
            key = jnp.where(left, kv0, pltpu.roll(kv1, 64, 1))
            value = jnp.where(left, pltpu.roll(kv0, 64, 1), kv1)
            mixed = jnp.where(left, pltpu.roll(row0, 64, 1), row1)
            project_grad[rows, at : at + 128] = turn(query, cos, low, high).astype(BF)
            project_grad[rows, 256 + at : 384 + at] = turn(key, cos, low, high).astype(BF)
            project_grad[rows, 512 + at : 640 + at] = value.astype(BF)
            mixed_out[rows, at : at + 128] = mixed.astype(BF)

    small[...] = jnp.zeros_like(small)
    for k in range(32):
        small[0, k // 2, k % 2 : k % 2 + 1, :] = early[k : k + 1, :]

    def keep(first, sums):
        for n in range(sums.shape[1] // 128):
            k = first + n
            small[1, k // 2, k % 2 : k % 2 + 1, :] = sums[:, n * 128 : n * 128 + 128]

    for copy in copies:
        copy.wait()
    gain_sums = jnp.zeros((1, 1024), F32)
    shift_sums = jnp.zeros((1, 1024), F32)
    bias_sums = jnp.zeros((1, 768), F32)
    normed_grad[:, here] = mm(project_grad[...], weight_here[...], NT)
    normed_grad[:, mine] = mm(project_grad[...], weight_mine[...], NT)
    normed_grad[:, others] = mm(project_grad[...], weight_other[...], NT)
    for block in range(4):
        rows = pl.ds(block * 128, 128)
        grads = project_grad[rows, :]
        entry = normed_grad[rows, :]
        gain_sums += jnp.sum(entry * xhat[rows, :].astype(F32), axis=0, keepdims=True)
        shift_sums += jnp.sum(entry, axis=0, keepdims=True)
        bias_sums += jnp.sum(grads.astype(F32), axis=0, keepdims=True)
    keep(0, gain_sums)
    keep(8, shift_sums)
    keep(16, bias_sums)

    for flip, target in ((0, out_own), (1, out_other)):
        to_core = core ^ flip
        for part in range(2):
            columns = normed[:, pl.ds(mult(part * 512 + to_core * 256, 256), 256)]
            for block in range(3):
                grads = mm(columns, project_grad[:, block * 256 : block * 256 + 256], TN).astype(BF)
                for n in range(2):
                    slot = part * 6 + block * 2 + n
                    target[:, slot * 16 : slot * 16 + 16, :] = grads[:, n * 128 : n * 128 + 128].reshape(
                        16, 16, 128
                    )
        for block in range(2):
            columns = upstream[:, pl.ds(mult(to_core * 512 + block * 256, 256), 256)]
            grads = mm(mixed_out[...], columns, TN).astype(BF)
            for n in range(2):
                at = 192 + (block * 2 + n) * 16
                target[:, at : at + 16, :] = grads[:, n * 128 : n * 128 + 128].reshape(16, 16, 128)
        target[:, 256:272, :] = small[to_core].astype(BF)


def feed_kernel(
    place, gains, vector, normed, upstream, xhat, weight, weight_mine, weight_other, proj,
    out_own, out_other, branch, entry, early, active, inner_grad, sums, weight_here, proj_here, sems,
):
    core, chip, half_in, low_x = place[0], place[1], place[2], place[3]
    here, mine, others = halves(half_in, core)
    copies = fetch(
        [
            (weight.at[:, pl.ds(mult(chip * 1024, 1024), 1024)], weight_here, sems.at[0]),
            (proj.at[pl.ds(mult(low_x * 1024, 1024), 1024), :], proj_here, sems.at[1]),
        ]
    )
    bias = jnp.concatenate([vector[pl.ds(28 + low_x * 8 + n, 1), :] for n in range(8)], axis=1)
    sums[...] = jnp.zeros_like(sums)
    sums[2:3, :] = jnp.sum(upstream[0:128, :].astype(F32), axis=0, keepdims=True)
    copies[0].wait()
    for block in range(2):
        rows = pl.ds(block * 256, 256)
        inner = (
            mm(normed[rows, here], weight_here[...])
            + mm(normed[rows, mine], weight_mine[...])
            + mm(normed[rows, others], weight_other[...])
            + bias
        )
        bell = 0.5 * (1.0 + lax.erf(inner * (2.0**-0.5)))
        act = (inner * bell).astype(BF)
        active[rows, :] = act
        if block == 0:
            copies[1].wait()
        branch[rows, :] = mm(act, proj_here[...])
        slope = bell + inner * jnp.exp(-0.5 * inner * inner) * (1.0 / math.sqrt(2.0 * math.pi))
        grad = (mm(upstream[rows, :], proj_here[...], NT) * slope).astype(BF)
        inner_grad[rows, :] = grad
        sums[3:4, :] += jnp.sum(grad.astype(F32), axis=0, keepdims=True)
        for cut, part in ((here, weight_here), (mine, weight_mine), (others, weight_other)):
            back = mm(grad, part[...], NT)
            entry[rows, cut] = back * gains[2:3, cut]
            sums[0:1, cut] += jnp.sum(back * xhat[rows, cut].astype(F32), axis=0, keepdims=True)
            sums[1:2, cut] += jnp.sum(back, axis=0, keepdims=True)
    for k in range(32):
        at = (k % 8) * 128
        early[k : k + 1, :] = sums[k // 8 : k // 8 + 1, at : at + 128]

    for flip, target in ((0, out_own), (1, out_other)):
        to_core = core ^ flip
        for part in range(2):
            features = normed[:, pl.ds(mult(part * 512 + to_core * 256, 256), 256)]
            for quad in range(4):
                grads = mm(features, inner_grad[:, quad * 256 : quad * 256 + 256], TN).astype(BF)
                for n in range(2):
                    slot = part * 8 + quad * 2 + n
                    target[:, slot * 16 : slot * 16 + 16, :] = grads[:, n * 128 : n * 128 + 128].reshape(
                        16, 16, 128
                    )
        features = active[:, pl.ds(mult(to_core * 512, 512), 512)]
        for quad in range(4):
            grads = mm(features, upstream[:, quad * 256 : quad * 256 + 256], TN).astype(BF)
            for n in range(2):
                at = 256 + (quad * 2 + n) * 32
                target[:, at : at + 32, :] = grads[:, n * 128 : n * 128 + 128].reshape(16, 32, 128)


def combine_kernel(own, arrived, out):
    out[:, 0:256, :] = (own[:, 0:256, :].astype(F32) + arrived[:, 0:256, :].astype(F32)).astype(BF)
    out[:, 256:320, :] = own[:, 256:320, :]
    out[:, 320:384, :] = arrived[:, 256:320, :]


def rows_kernel(place, branch, mixed, out_weight, normed_grad, entry, gains, *outs):
    weight = out_weight[pl.ds(mult(place[3] * 256, 256), 256), :]
    for block, out in enumerate(outs):
        rows = pl.ds(block * 128, 128)
        out[0:128, :] = (branch[rows, :] + mm(mixed[rows, :], weight)).astype(BF)
        out[128:256, :] = (normed_grad[rows, :] * gains[0:1, :] + entry[rows, :]).astype(BF)


def sums_kernel(
    place, own, other, attn_gain, attn_shift, mlp_gain, mlp_shift, out_bias, qkv_bias, in_bias,
    parts, totals, columns,
):
    core, chip, half_in, low_x = place[0], place[1], place[2], place[3]
    for flip, source in ((0, own), (1, other)):
        for behind in range(4):
            part = source[:, behind * 16 : behind * 16 + 16, :].astype(F32)[:, 0:2, :]
            parts[core ^ flip, behind] = part.reshape(32, 128)
    for part in range(2):
        totals[part] = (parts[part, 0] + parts[part, 1]) + (parts[part, 2] + parts[part, 3])
    for part, first, out in (
        (1, 0, attn_gain), (1, 8, attn_shift), (0, 0, mlp_gain), (0, 8, mlp_shift), (0, 16, out_bias),
    ):
        out[...] = totals[part, pl.ds(first + half_in * 4, 4), :]
    for behind in range(4):
        origin = (chip + 4 - behind) % 4
        for k in range(3):
            columns[pl.ds(k * 8 + origin * 2, 2), :] = parts[1, behind, 16 + k * 2 : 18 + k * 2, :]
    qkv_bias[...] = columns[pl.ds(half_in * 12, 12), :]
    in_bias[pl.ds(mult(low_x * 8, 8), 8), :] = parts[0, 0, 24:32, :]
    in_bias[pl.ds(mult(8 - low_x * 8, 8), 8), :] = parts[0, 3 - low_x * 2, 24:32, :]


def finish_kernel(
    place, hidden, upstream, rows0, rows1, rows2, rows3, vector, vector_other, hidden_out, hidden_grad, bias
):
    half_in = place[2]
    bias[:, pl.ds(mult(half_in * 512, 512), 512)] = wide_row(vector, 44, 4) + wide_row(vector, 48, 4)
    bias[:, pl.ds(mult(512 - half_in * 512, 512), 512)] = wide_row(vector_other, 44, 4) + wide_row(vector_other, 48, 4)
    shares = [part.astype(F32) for part in (rows0[...], rows1[...], rows2[...], rows3[...])]
    total = (shares[0] + shares[1]) + (shares[2] + shares[3])
    full = hidden[...].astype(F32)
    hidden_out[...] = (full + total[:128] + bias[...]).astype(BF)
    xhat, scale = normalized(full)
    entry = total[128:]
    hidden_grad[...] = upstream[...].astype(F32) + scale * (
        entry
        - jnp.mean(entry, axis=1, keepdims=True)
        - xhat * jnp.mean(entry * xhat, axis=1, keepdims=True)
    )


def spread_kernel(place, piece, out, *, columns):
    for behind, slot, rows, step, at in columns:
        start = at
        if step:
            start = mult(at + ((place[1] + 4 - behind) % 4) * step, 128)
        part = piece[:, slot : slot + rows, :].astype(F32)
        out[:, pl.ds(start, 128)] = part.reshape(piece.shape[0] * rows, 128)


def spread(place, pieces, at_rows, shape_out, block, grid, in_map, out_map, columns):
    return pl.pallas_call(
        functools.partial(spread_kernel, columns=columns),
        out_shape=jax.ShapeDtypeStruct(shape_out, F32),
        grid_spec=pltpu.PrefetchScalarGridSpec(
            num_scalar_prefetch=1,
            grid=grid,
            in_specs=[pl.BlockSpec((8, at_rows, 128), in_map)],
            out_specs=pl.BlockSpec(block, out_map),
        ),
        compiler_params=pltpu.CompilerParams(vmem_limit_bytes=60 * MIB),
    )(place, pieces)


def heads_spread_kernel(place, piece, *refs):
    qkv, out = refs[-2:]
    for behind in range(4):
        start = ((place[1] + 4 - behind) % 4) * 256
        for n in range(6):
            slot = behind * 96 + n * 16
            at = mult((n // 2) * 1024 + (n % 2) * 128 + start, 128)
            qkv[:, pl.ds(at, 128)] = piece[:, slot : slot + 16, :].astype(F32).reshape(128, 128)
    for flip in range(2):
        for n in range(4):
            slot = 384 + flip * 64 + n * 16
            out[place[3] ^ flip, :, n * 128 : n * 128 + 128] = (
                piece[:, slot : slot + 16, :].astype(F32).reshape(128, 128)
            )


def heads_spread(place, pieces, flip, before=()):
    return pl.pallas_call(
        heads_spread_kernel,
        out_shape=[shape(512, 3072, dtype=F32), shape(2, 256, 1024, dtype=F32)],
        grid_spec=pltpu.PrefetchScalarGridSpec(
            num_scalar_prefetch=1,
            grid=(2,),
            in_specs=[pl.BlockSpec((8, 576, 128), lambda g, place: (g, 0, 0))]
            + [pl.BlockSpec(memory_space=pl.ANY) for _ in before],
            out_specs=[
                pl.BlockSpec((128, 3072), lambda g, place: ((place[0] ^ flip) * 2 + g, 0)),
                pl.BlockSpec((2, 128, 512), lambda g, place: (0, g, place[0] ^ flip)),
            ],
        ),
        input_output_aliases={2 + k: k for k in range(len(before))},
        compiler_params=pltpu.CompilerParams(vmem_limit_bytes=60 * MIB),
    )(place, pieces, *before)


def shape(*sizes, dtype=BF):
    return jax.ShapeDtypeStruct(sizes, dtype)


def normalized(hidden):
    moved = hidden - jnp.mean(hidden, axis=-1, keepdims=True)
    spread_out = jnp.mean(moved * moved, axis=-1, keepdims=True)
    scale = lax.rsqrt(spread_out + EPS)
    return moved * scale, scale


def per_device(
    hidden_in, doc_ids, block_map, attn_gain, attn_shift, mlp_gain, mlp_shift, qkv_weight, qkv_bias,
    out_weight, out_bias, in_weight, in_bias, proj_weight, proj_bias, cotangent,
):
    y, z = lax.axis_index("y"), lax.axis_index("z")
    xh, xl = lax.axis_index("xh"), lax.axis_index("xl")
    core = lax.axis_index("core")
    group = y * 4 + z
    chip = xh * 2 + xl
    low_half = xh == 0
    smem = whole(pltpu.SMEM)
    place = jnp.stack([core, chip, xh, xl, group]).astype(jnp.int32)

    partner = 3 - chip
    piece = jnp.concatenate(
        [
            lax.dynamic_slice(qkv_weight, (core * 256, k * 1024 + partner * 256), (256, 256))
            for k in range(3)
        ],
        axis=1,
    )
    payload = jnp.stack([hidden_in[0], cotangent[0]])
    frequency = 10000.0 ** (-(jnp.arange(0, ROT, 2).astype(F32) / ROT))
    lanes = jnp.concatenate([frequency, frequency, jnp.zeros((48,), F32)])
    lanes = jnp.concatenate([lanes, lanes])[None]
    bounds = [jnp.sum((doc_ids < label).astype(F32)).reshape(1) for label in (1, 2)]
    parts = (attn_gain, attn_shift, mlp_gain, mlp_shift, qkv_bias, in_bias, out_bias, proj_bias, *bounds)
    vector, at = jnp.zeros((7168,), F32), 0
    for part in parts:
        vector = vector + lax.pad(part.astype(F32), jnp.float32(0), [(at, 7168 - at - part.shape[0], 0)])
        at += part.shape[0]
    vector = vector.reshape(56, 128)
    piece, payload, place, lanes = lax.optimization_barrier((piece, payload, place, lanes))
    qkv_mine = cross(piece)
    qkv_other = swap(qkv_mine, "core")
    ring = [payload] + [shift_ring(payload, d) for d in (1, 2, 3)]
    in_piece = lax.dynamic_slice(in_weight, (core * 256, partner * 1024), (256, 1024))
    vector, in_piece = lax.optimization_barrier((vector, in_piece))
    vector_other = cross(vector)

    in_mine = cross(in_piece)
    in_mine, in_other = held(in_mine, swap(in_mine, "core"))

    send, normed, normed_mlp, xhat, upstream, cosine, sine, gains = call(
        project_kernel,
        [shape(16, 384, 128)]
        + [shape(512, 1024)] * 4
        + [shape(512, 128, dtype=F32)] * 2
        + [shape(4, 1024, dtype=F32)],
        [smem] * 2 + [whole()] * 7 + [whole(pl.ANY)] + [whole()] * 2 + [whole(pl.ANY)],
        scratch=[
            pltpu.VMEM((512, 768), BF),
            pltpu.VMEM((256, 1024), BF),
            pltpu.SemaphoreType.DMA((4,)),
        ],
    )(
        place, block_map, *ring, vector, vector_other, lanes, qkv_weight, qkv_mine, qkv_other, out_weight
    )
    heads_own = lax.all_to_all(send, PLANE, 0, 0, tiled=True)

    feed_own, feed_other, branch, entry, early = call(
        feed_kernel,
        [shape(16, 512, 128)] * 2 + [shape(512, 1024, dtype=F32)] * 2 + [shape(32, 128, dtype=F32)],
        [smem] + [whole()] * 5 + [whole(pl.ANY)] + [whole()] * 2 + [whole(pl.ANY)],
        scratch=[pltpu.VMEM((512, 1024), BF)] * 2
        + [
            pltpu.VMEM((4, 1024), F32),
            pltpu.VMEM((512, 1024), BF),
            pltpu.VMEM((1024, 1024), BF),
            pltpu.SemaphoreType.DMA((2,)),
        ],
    )(place, gains, vector, normed_mlp, upstream, xhat, in_weight, in_mine, in_other, proj_weight)
    feed_both = feed_own + swap(feed_other, "core")

    def reduce_plane(both):
        parts = lax.all_to_all(both, PLANE, 0, 0, tiled=True)
        return jnp.sum(parts.astype(F32), axis=0)

    def around(parts, rest=()):
        got = [jnp.concatenate([lax.dynamic_index_in_dim(parts, xh, 0, False), *rest])]
        for d in (1, 2, 3):
            half = ((chip + d) % 4) // 2
            got.append(
                shift_ring(jnp.concatenate([lax.dynamic_index_in_dim(parts, half, 0, False), *rest]), d)
            )
        return got

    heads_other = swap(heads_own, "core")
    heads_own, heads_other, feed_both, early, entry, branch = lax.optimization_barrier(
        (heads_own, heads_other, feed_both, early, entry, branch)
    )
    feed = reduce_plane(feed_both)
    quarter = (group % 2) * 2 + core
    bounds = jnp.where(group // 8 == xh, vector[52, :2], vector_other[52, :2])
    spot = jnp.concatenate([jnp.stack([core, quarter]).astype(jnp.int32), bounds.astype(jnp.int32)])
    back_own, back_other = call(
        attend_kernel,
        [shape(16, 320, 128)] * 2,
        [smem, smem] + [whole()] * 2,
        scratch=attend_scratch(),
        flops=45 * 10**9,
        moved=6 * MIB,
    )(spot, block_map, heads_own, heads_other)

    (returning,) = call(combine_kernel, [shape(16, 384, 128)], [whole()] * 2, limit=16)(
        back_own, swap(back_other, "core")
    )
    feed = feed.astype(BF)
    in_parts = around(feed[:256].reshape(2, 128, 128))
    proj_parts = [feed[256:], swap(feed[256:], "xl")]
    *feed_parts, returning = lax.optimization_barrier((*in_parts, *proj_parts, returning))
    feed_parts, returning = lax.optimization_barrier((jnp.concatenate(feed_parts), returning))
    feed_all = lax.all_gather(feed_parts, ("core",) + PLANE, axis=0)
    returned = lax.all_to_all(returning, PLANE, 0, 0, tiled=True)
    heads_grad_own, heads_grad_other, normed_grad, project_grad, mixed = call(
        return_kernel,
        [shape(16, 272, 128)] * 2 + [shape(512, 1024, dtype=F32), shape(512, 768), shape(512, 256)],
        [smem] + [whole()] * 6 + [whole(pl.ANY)] + [whole()] * 3,
        scratch=[
            pltpu.VMEM((2, 128, 128), BF),
            pltpu.VMEM((2, 16, 16, 128), F32),
            pltpu.VMEM((512, 768), BF),
            pltpu.SemaphoreType.DMA((3,)),
        ],
    )(place, returned, cosine, sine, normed, xhat, upstream, qkv_weight, qkv_mine, qkv_other, early)
    heads_both = heads_grad_own + swap(heads_grad_other, "core")
    heads_sum = reduce_plane(heads_both).astype(BF)

    to_rows = call(rows_kernel, [shape(256, 1024)] * 4, [smem] + [whole()] * 6, limit=20)(
        place, branch, mixed, out_weight, normed_grad, entry, gains
    )
    heads_sum, *to_rows = lax.optimization_barrier((heads_sum, *to_rows))

    heads_parts = around(heads_sum[:192].reshape(2, 96, 128), (heads_sum[256:], heads_sum[192:256]))
    beside = jnp.where(xl == 0, heads_parts[3], heads_parts[1])
    gathering = jnp.concatenate(
        [part[:96] for part in heads_parts]
        + [heads_parts[0][112:], beside[112:]]
        + [part[96:112] for part in heads_parts]
    )
    gathering, *to_rows = lax.optimization_barrier((gathering, *to_rows))
    heads_all = to_all(gathering, PLANE, 16)

    arrived = [to_rows[0]] + [shift_ring(to_rows[d], 4 - d) for d in (1, 2, 3)]
    in_weight_grad = spread(
        place, feed_all, 512, (512, 4096), (128, 4096), (4,),
        lambda g, place: (g, 0, 0), lambda g, place: (g, 0),
        [(c, c * 128 + n * 16, 16, 1024, n * 128) for c in range(4) for n in range(8)],
    )
    proj_weight_grad = spread(
        place, feed_all, 256, (2048, 1024), (256, 1024), (2, 4),
        lambda a, g, place: (g, 2 + a, 0), lambda a, g, place: ((place[3] ^ a) * 4 + g, 0),
        [(0, n * 32, 32, 0, n * 128) for n in range(8)],
    )
    heads_all, in_weight_grad, proj_weight_grad, *arrived = lax.optimization_barrier(
        (heads_all, in_weight_grad, proj_weight_grad, *arrived)
    )
    heads_core = swap(heads_all, "core")
    hidden_out, hidden_grad = call(
        finish_kernel,
        [shape(128, 1024), shape(128, 1024, dtype=F32)],
        [smem] + [whole()] * 8,
        scratch=[pltpu.VMEM((1, 1024), F32)],
        limit=16,
    )(place, hidden_in[0], cotangent[0], *arrived, vector, vector_other)
    hidden_out, hidden_grad = hidden_out[None], hidden_grad[None]

    sums = call(
        sums_kernel,
        [shape(rows, 128, dtype=F32) for rows in (4, 4, 4, 4, 4, 12, 16)],
        [smem] + [pl.BlockSpec((16, 64, 128), lambda g: (0, 8, 0))] * 2,
        scratch=[pltpu.VMEM((2, 4, 32, 128), F32), pltpu.VMEM((2, 32, 128), F32), pltpu.VMEM((24, 128), F32)],
        grid=(1,),
    )(place, heads_all, heads_core)
    (
        attn_gain_grad, attn_shift_grad, mlp_gain_grad, mlp_shift_grad, out_bias_grad, qkv_bias_grad,
        in_bias_grad,
    ) = [part.reshape(-1) for part in sums]

    partial = heads_spread(place, heads_all, 0)
    qkv_weight_grad, out_weight_grad = heads_spread(place, heads_core, 1, partial)
    out_weight_grad = out_weight_grad.reshape(512, 1024)

    return (
        hidden_out, hidden_grad, attn_gain_grad, attn_shift_grad, mlp_gain_grad, mlp_shift_grad,
        qkv_weight_grad, qkv_bias_grad, out_weight_grad, out_bias_grad, in_weight_grad, in_bias_grad,
        proj_weight_grad, out_bias_grad,
    )


def solution(mesh):
    fine = Mesh(mesh.devices.reshape(4, 4, 2, 2, 2), ("y", "z", "xl", "core", "xh"))
    ctx = ("y", "z", "xl", "core")
    rows = P("xh", ctx, None)
    half = P("xh")
    wide = P("xh", None)
    in_specs = (
        rows, wide, P(), half, half, half, half, wide, half, wide, half, wide, half, wide, half, rows,
    )
    out_specs = (
        rows, rows, half, half, half, half, wide, half, wide, half, wide, half, wide, half,
    )
    return jax.shard_map(
        per_device, mesh=fine, in_specs=in_specs, out_specs=out_specs, check_vma=False
    )
```

```python
import functools
import math

import jax
import jax.numpy as jnp
from jax import lax
from jax.experimental import pallas as pl
from jax.experimental.pallas import tpu as pltpu
from jax.sharding import Mesh
from jax.sharding import PartitionSpec as P

ROT = 16
EPS = 1e-05
NEG_FILL = -1e30
BF = jnp.bfloat16
F32 = jnp.float32
RING = ("xh", "xl")
PLANE = ("y", "z")
MIB = 1 << 20

NN = (((1,), (0,)), ((), ()))
NT = (((1,), (1,)), ((), ()))
TN = (((0,), (0,)), ((), ()))


def mm(left, right, dims=NN):
    return lax.dot_general(left, right, dims, preferred_element_type=F32)


def mult(value, step):
    return pl.multiple_of(value, step)


def whole(space=pltpu.VMEM):
    return pl.BlockSpec(memory_space=space)


def call(body, outs, ins, scratch=(), flops=0, moved=0, limit=60, grid=()):
    return pl.pallas_call(
        body,
        out_shape=outs,
        grid=grid,
        in_specs=ins,
        out_specs=[whole() for _ in outs],
        scratch_shapes=list(scratch),
        cost_estimate=pl.CostEstimate(flops=flops, bytes_accessed=moved, transcendentals=0),
        compiler_params=pltpu.CompilerParams(vmem_limit_bytes=limit * MIB),
    )


def held(*arrays):
    return pl.pallas_call(
        lambda *refs: None,
        out_shape=[jax.ShapeDtypeStruct(a.shape, a.dtype) for a in arrays],
        in_specs=[whole(pl.ANY) for _ in arrays],
        out_specs=[whole(pl.ANY) for _ in arrays],
        input_output_aliases={k: k for k in range(len(arrays))},
        cost_estimate=pl.CostEstimate(flops=4 * 10**9, bytes_accessed=0, transcendentals=0),
    )(*arrays)


def to_all(array_in, axes, count):
    copies = jnp.broadcast_to(array_in[None], (count,) + array_in.shape)
    return lax.all_to_all(copies, axes, 0, 0, tiled=True)


def swap(array_in, axis):
    return lax.ppermute(array_in, axis, [(0, 1), (1, 0)])


def shift_ring(array_in, places):
    spots = [(x % 2) * 2 + x // 2 for x in range(4)]
    return lax.ppermute(
        array_in, ("xl", "xh"), [(spots[x], spots[(x + places) % 4]) for x in range(4)]
    )


def cross(array_in):
    return lax.ppermute(array_in, ("xl", "xh"), [(0, 3), (1, 2), (2, 1), (3, 0)])


def in_order(first, mine, other):
    return jnp.where(first, jnp.stack([mine, other]), jnp.stack([other, mine]))


def turn(tile, cosine, sine_low, sine_high):
    return (
        tile * cosine
        + pltpu.roll(tile, 120, 1) * sine_low
        + pltpu.roll(tile, 8, 1) * sine_high
    )


def sine_parts(sine, sign):
    spot = lax.broadcasted_iota(jnp.int32, sine.shape, 1) % 64
    low = jnp.where(spot < 8, -sign * sine, 0.0)
    high = jnp.where((spot >= 8) & (spot < 16), sign * sine, 0.0)
    return low, high


def wide_row(vector, first, count):
    return jnp.concatenate([vector[first + k : first + k + 1, :] for k in range(count)], axis=1)


def halves(half_in, core):
    start = 512 - half_in * 512
    return (
        pl.ds(mult(half_in * 512, 512), 512),
        pl.ds(mult(start + core * 256, 256), 256),
        pl.ds(mult(start + 256 - core * 256, 256), 256),
    )


def fetch(copies):
    started = [pltpu.make_async_copy(*copy) for copy in copies]
    for copy in started:
        copy.start()
    return started


def qkv_copies(place, weight, mine, other, target, sems):
    core, chip, half_in = place[0], place[1], place[2]
    here = pl.ds(mult(half_in * 512, 512), 512)
    away = 512 - half_in * 512
    return [
        (
            weight.at[:, pl.ds(mult(k * 1024 + chip * 256, 256), 256)],
            target.at[here, pl.ds(k * 256, 256)],
            sems.at[k],
        )
        for k in range(3)
    ] + [
        (mine, target.at[pl.ds(mult(away + core * 256, 256), 256), :], sems.at[3]),
        (other, target.at[pl.ds(mult(away + 256 - core * 256, 256), 256), :], sems.at[4]),
    ]


def project_kernel(
    place, block_map, rows0, rows1, rows2, rows3, vector, vector_other, lanes, weight, weight_mine,
    weight_other, out_weight, send, normed, normed_mlp, xhat, upstream, cosine, sine, gains,
    weight_here, out_here, sems,
):
    own_core, chip, half_in, low_x, group = place[0], place[1], place[2], place[3], place[4]
    here = pl.ds(mult(half_in * 512, 512), 512)
    copies = fetch(
        qkv_copies(place, weight, weight_mine, weight_other, weight_here, sems)
        + [(out_weight.at[pl.ds(mult(low_x * 256, 256), 256), :], out_here, sems.at[5])]
    )
    there = pl.ds(mult(512 - half_in * 512, 512), 512)
    for k in range(4):
        gains[k : k + 1, here] = wide_row(vector, k * 4, 4)
        gains[k : k + 1, there] = wide_row(vector_other, k * 4, 4)
    left = lax.broadcasted_iota(jnp.int32, (64, 128), 1) < 64
    left_all = lax.broadcasted_iota(jnp.int32, (128, 128), 1) < 64
    row = lax.broadcasted_iota(jnp.int32, (128, 1), 0)

    def pack(tile):
        low, high = tile[:64], tile[64:]
        return (
            jnp.where(left, low, pltpu.roll(high, 64, 1)).astype(BF),
            jnp.where(left, pltpu.roll(low, 64, 1), high).astype(BF),
        )

    def bias_of(k):
        at = k * 1024 + chip * 256
        spot = 16 + (at % 1536) // 128
        parts = [
            jnp.where(at // 1536 == half_in, vector[pl.ds(spot + n, 1), :], vector_other[pl.ds(spot + n, 1), :])
            for n in range(2)
        ]
        return jnp.concatenate(parts, axis=1)

    biases = [bias_of(k) for k in range(3)]
    for copy in copies:
        copy.wait()
    for back, source in enumerate((rows0, rows1, rows2, rows3)):
        origin = (chip + 4 - back) % 4
        stream, half_x = origin // 2, origin % 2
        rows = pl.ds(back * 128, 128)
        moved = source[0].astype(F32)
        moved = moved - jnp.mean(moved, axis=1, keepdims=True)
        spread = jnp.mean(moved * moved, axis=1, keepdims=True)
        unit = moved * lax.rsqrt(spread + EPS)
        xhat[rows, :] = unit.astype(BF)
        normed[rows, :] = (unit * gains[0:1, :] + gains[1:2, :]).astype(BF)
        normed_mlp[rows, :] = (unit * gains[2:3, :] + gains[3:4, :]).astype(BF)
        upstream[rows, :] = source[1]

        block = block_map[(group * 2 + half_x) * 2 + own_core]
        position = jnp.where(row < 64, block * 64 + row, (127 - block) * 64 + row - 64).astype(F32)
        same = stream == half_in
        second = jnp.where(same, vector[52:53, 0:1], vector_other[52:53, 0:1])
        third = jnp.where(same, vector[52:53, 1:2], vector_other[52:53, 1:2])
        first = jnp.where(position >= third, third, jnp.where(position >= second, second, 0.0))
        angles = (position - first) * lanes[...]
        cos, sin = jnp.cos(angles), jnp.sin(angles)
        cosine[rows, :] = cos
        sine[rows, :] = sin
        low, high = sine_parts(sin, 1.0)

        project = mm(normed[rows, :], weight_here[...])
        queries, keys, values = [project[:, k * 256 : k * 256 + 256] + biases[k] for k in range(3)]
        grads = mm(source[1], out_here[...], NT)
        for pair in range(2):
            at = pair * 128
            query = pack(turn(queries[:, at : at + 128], cos, low, high) * 0.125)
            grad = pack(grads[:, at : at + 128])
            key = turn(keys[:, at : at + 128], cos, low, high)
            value = values[:, at : at + 128]
            key_value = (
                jnp.where(left_all, key, pltpu.roll(value, 64, 1)).astype(BF),
                jnp.where(left_all, pltpu.roll(key, 64, 1), value).astype(BF),
            )
            for member in range(2):
                for half in range(2):
                    target = stream * 8 + (pair * 2 + member) * 2 + half
                    send[target, pl.ds(mult(half_x * 128, 128), 128), :] = key_value[member]
                    for core in range(2):
                        quarter = half * 2 + core
                        cut = slice(quarter * 16, quarter * 16 + 16)
                        spot = core * 32 + half_x * 16
                        send[target, pl.ds(mult(256 + spot, 16), 16), :] = query[member][cut]
                        send[target, pl.ds(mult(320 + spot, 16), 16), :] = grad[member][cut]


ROWS = 256
KEYS = 1024
STRAIGHT = (2, 3, 4, 5)


def attend_scratch():
    return [
        pltpu.VMEM((8192, 128), BF),
        pltpu.VMEM((2048, 128), BF),
        pltpu.VMEM((ROWS, 8192), F32),
        pltpu.VMEM((ROWS, 8192), BF),
        pltpu.VMEM((128, 8192), F32),
        pltpu.VMEM((2048, 128), BF),
    ]


def attend_kernel(
    place, block_map, own, other, out_own, out_other, kv, q_grad, scores, chances, key_sums, rows_out,
):
    core, quarter, second, third = place[0], place[1], place[2], place[3]
    left16 = lax.broadcasted_iota(jnp.int32, (16, 128), 1) < 64
    left = lax.broadcasted_iota(jnp.int32, (ROWS, 128), 1) < 64

    def blocks_of(from_core, body):
        @pl.loop(0, 8)
        def _(step):
            for unrolled in range(4):
                i = step * 4 + unrolled
                block = block_map[i * 2 + from_core]
                body(i // 2, i % 2, block, 127 - block)

    def fill(source, from_core):
        def body(group, half_x, block, mirror):
            for upper, to in ((0, block), (1, mirror)):
                kv[pl.ds(mult(to * 64, 64), 64), :] = source[
                    group, pl.ds(mult(half_x * 128 + upper * 64, 64), 64), :
                ]
            spot = core * 32 + half_x * 16
            query = source[group, pl.ds(mult(256 + spot, 16), 16), :].astype(F32)
            grad = source[group, pl.ds(mult(320 + spot, 16), 16), :].astype(F32)
            q_grad[pl.ds(mult(block * 16, 16), 16), :] = jnp.where(
                left16, query, pltpu.roll(grad, 64, 1)
            ).astype(BF)
            q_grad[pl.ds(mult(mirror * 16, 16), 16), :] = jnp.where(
                left16, pltpu.roll(query, 64, 1), grad
            ).astype(BF)

        blocks_of(from_core, body)

    fill(own, core)
    fill(other, 1 - core)
    key_sums[...] = jnp.zeros_like(key_sums)

    row = lax.broadcasted_iota(jnp.int32, (ROWS, 1), 0)
    offset = (row // 16) * 64 + quarter * 16 + row % 16

    def start_of(position):
        return jnp.where(position >= third, third, jnp.where(position >= second, second, 0))

    def join(first_row, old, new):
        return new if first_row == 0 else jnp.concatenate([old[:first_row], new], axis=0)

    def work(tile):
        rows = pl.ds(mult(tile * ROWS, ROWS), ROWS)
        base = tile * KEYS
        both = q_grad[rows, :]
        position = base + offset
        start = start_of(position)
        query = jnp.where(left, both, jnp.zeros_like(both))

        def whole_cut(j, masked):
            return (j * KEYS, KEYS, 0, masked and "start")

        diagonal = [(base, KEYS // 2, 0, "causal"), (base + KEYS // 2, KEYS // 2, ROWS // 2, "causal")]

        def keys_of(cut):
            return pl.ds(mult(cut[0], KEYS // 2), cut[1])

        def score(cut, top):
            first_key, width, first_row, masked = cut
            part = mm(query[first_row:], kv[keys_of(cut), :], NT)
            if masked:
                spots = lax.broadcasted_iota(jnp.int32, part.shape, 1)
                allowed = spots >= start[first_row:] - first_key
                if masked == "causal":
                    allowed &= spots <= position[first_row:] - first_key
                part = jnp.where(allowed, part, NEG_FILL)
            scores[first_row:, keys_of(cut)] = part
            best = top[first_row:]
            for c in range(width // 128):
                best = jnp.maximum(best, part[:, c * 128 : c * 128 + 128])
            return join(first_row, top, best)

        def weigh(cut, row_top, total, mixed):
            _, width, first_row, _ = cut
            part = jnp.exp(scores[first_row:, keys_of(cut)] - row_top[first_row:])
            sums = total[first_row:]
            for c in range(width // 128):
                sums = sums + part[:, c * 128 : c * 128 + 128]
            rounded = part.astype(BF)
            chances[first_row:, keys_of(cut)] = rounded
            values = mixed[first_row:] + mm(rounded, kv[keys_of(cut), :])
            return join(first_row, total, sums), join(first_row, mixed, values)

        def back(cut, grad, delta, query_turned, grad_turned, query_sum):
            _, _, first_row, _ = cut
            keys = keys_of(cut)
            part = chances[first_row:, keys]
            along = mm(grad[first_row:], kv[keys, :], NT)
            score_grad = (part.astype(F32) * (along - delta[first_row:])).astype(BF)
            key_sums[0:64, keys] += mm(query_turned[:, first_row:], score_grad)
            key_sums[64:128, keys] += mm(grad_turned[:, first_row:], part)
            sums = query_sum[first_row:] + mm(score_grad, kv[keys, :])
            return join(first_row, query_sum, sums)

        def passes(first, last, middle, cuts):
            zero = jnp.zeros((ROWS, 128), F32)
            top = jnp.full((ROWS, 128), NEG_FILL, F32)
            if first is not None:
                top = lax.fori_loop(first, middle, lambda j, v: score(whole_cut(j, True), v), top)
                top = lax.fori_loop(middle, last, lambda j, v: score(whole_cut(j, False), v), top)
            for cut in cuts:
                top = score(cut, top)
            row_top = jnp.max(top, axis=1, keepdims=True)
            state = (zero, zero)
            if first is not None:
                state = lax.fori_loop(
                    first, last, lambda j, v: weigh(whole_cut(j, False), row_top, *v), state
                )
            for cut in cuts:
                state = weigh(cut, row_top, *state)
            total, mixed = state
            share = 1.0 / jnp.sum(total, axis=1, keepdims=True)
            mixed = mixed * share
            scaled = jnp.where(left, both.astype(F32), both.astype(F32) * share)
            grad = jnp.where(left, 0.0, scaled)
            delta = jnp.sum(grad * mixed, axis=1, keepdims=True)
            grad = grad.astype(BF)
            turned = scaled.T.astype(BF)
            fixed_part = (grad, delta, turned[:64], turned[64:])
            query_sum = zero
            if first is not None:
                query_sum = lax.fori_loop(
                    first, last, lambda j, v: back(whole_cut(j, False), *fixed_part, v), query_sum
                )
            for cut in cuts:
                query_sum = back(cut, *fixed_part, query_sum)
            rows_out[rows, :] = jnp.where(left, query_sum * 0.125, mixed).astype(BF)

        low = jnp.minimum(start_of(base + quarter * 16) // KEYS, tile)
        count = tile + 1 - low
        usual = (count >= STRAIGHT[0]) & (count <= STRAIGHT[-1])
        for n in STRAIGHT:

            @pl.when(count == n)
            def _(n=n):
                passes(None, None, None, [whole_cut(low + i, True) for i in range(n - 1)] + diagonal)

        @pl.when(jnp.logical_not(usual))
        def _():
            high = (start_of(base + KEYS - 64 + quarter * 16 + 15) + KEYS - 1) // KEYS
            passes(low, tile, jnp.minimum(jnp.maximum(high, low), tile), diagonal)

    pl.loop(0, 8)(work)

    @pl.loop(0, 8)
    def _(c):
        for d in range(8):
            cut = pl.ds(mult(c * 1024 + d * 128, 128), 128)
            kv[cut, :] = key_sums[:, cut].T.astype(BF)

    def spill(target, to_core):
        def body(group, half_x, block, mirror):
            spot = 256 + half_x * 32
            for upper, at in ((0, block), (1, mirror)):
                target[group, pl.ds(mult(half_x * 128 + upper * 64, 64), 64), :] = kv[
                    pl.ds(mult(at * 64, 64), 64), :
                ]
                target[group, pl.ds(mult(spot + upper * 16, 16), 16), :] = rows_out[
                    pl.ds(mult(at * 16, 16), 16), :
                ]

        blocks_of(to_core, body)

    spill(out_own, core)
    spill(out_other, 1 - core)


def return_kernel(
    place, back, cosine, sine, normed, xhat, upstream, weight, weight_mine,
    weight_other, early, out_own, out_other, normed_grad, project_grad, mixed_out, heads, small,
    weight_here, sems,
):
    core, chip = place[0], place[1]
    copies = fetch(qkv_copies(place, weight, weight_mine, weight_other, weight_here, sems))
    left = lax.broadcasted_iota(jnp.int32, (128, 128), 1) < 64
    for behind in range(4):
        origin = (chip + 4 - behind) % 4
        stream, half_x = origin // 2, origin % 2
        rows = pl.ds(behind * 128, 128)
        cos = cosine[rows, :]
        low, high = sine_parts(sine[rows, :], -1.0)
        for pair in range(2):
            pieces = []
            for member in range(2):
                base = stream * 8 + (pair * 2 + member) * 2
                cut = pl.ds(mult(half_x * 128, 128), 128)
                key_value = back[base, cut, :].astype(F32) + back[base + 1, cut, :].astype(F32)
                for upper in range(2):
                    for half in range(2):
                        for of_core in range(2):
                            flipped = of_core ^ core
                            spot = 256 + flipped * 64 + (half_x * 2 + upper) * 16
                            heads[
                                member, pl.ds(upper * 64 + (half * 2 + of_core) * 16, 16), :
                            ] = back[base + half, pl.ds(mult(spot, 16), 16), :]
                pieces.append((heads[member].astype(F32), key_value))
            (row0, kv0), (row1, kv1) = pieces
            at = pair * 128
            query = jnp.where(left, row0, pltpu.roll(row1, 64, 1))
            key = jnp.where(left, kv0, pltpu.roll(kv1, 64, 1))
            value = jnp.where(left, pltpu.roll(kv0, 64, 1), kv1)
            mixed = jnp.where(left, pltpu.roll(row0, 64, 1), row1)
            project_grad[rows, at : at + 128] = turn(query, cos, low, high).astype(BF)
            project_grad[rows, 256 + at : 384 + at] = turn(key, cos, low, high).astype(BF)
            project_grad[rows, 512 + at : 640 + at] = value.astype(BF)
            mixed_out[rows, at : at + 128] = mixed.astype(BF)

    small[...] = jnp.zeros_like(small)
    for k in range(32):
        small[0, k // 2, k % 2 : k % 2 + 1, :] = early[k : k + 1, :]

    def keep(first, sums):
        for n in range(sums.shape[1] // 128):
            k = first + n
            small[1, k // 2, k % 2 : k % 2 + 1, :] = sums[:, n * 128 : n * 128 + 128]

    for copy in copies:
        copy.wait()
    gain_sums = jnp.zeros((1, 1024), F32)
    shift_sums = jnp.zeros((1, 1024), F32)
    bias_sums = jnp.zeros((1, 768), F32)
    normed_grad[...] = mm(project_grad[...], weight_here[...], NT)
    for block in range(4):
        rows = pl.ds(block * 128, 128)
        grads = project_grad[rows, :]
        entry = normed_grad[rows, :]
        gain_sums += jnp.sum(entry * xhat[rows, :].astype(F32), axis=0, keepdims=True)
        shift_sums += jnp.sum(entry, axis=0, keepdims=True)
        bias_sums += jnp.sum(grads.astype(F32), axis=0, keepdims=True)
    keep(0, gain_sums)
    keep(8, shift_sums)
    keep(16, bias_sums)

    for flip, target in ((0, out_own), (1, out_other)):
        to_core = core ^ flip
        for part in range(2):
            columns = normed[:, pl.ds(mult(part * 512 + to_core * 256, 256), 256)]
            for block in range(3):
                grads = mm(columns, project_grad[:, block * 256 : block * 256 + 256], TN).astype(BF)
                for n in range(2):
                    slot = part * 6 + block * 2 + n
                    target[:, slot * 16 : slot * 16 + 16, :] = grads[:, n * 128 : n * 128 + 128].reshape(
                        16, 16, 128
                    )
        for block in range(2):
            columns = upstream[:, pl.ds(mult(to_core * 512 + block * 256, 256), 256)]
            grads = mm(mixed_out[...], columns, TN).astype(BF)
            for n in range(2):
                at = 192 + (block * 2 + n) * 16
                target[:, at : at + 16, :] = grads[:, n * 128 : n * 128 + 128].reshape(16, 16, 128)
        target[:, 256:272, :] = small[to_core].astype(BF)


def feed_kernel(
    place, gains, vector, normed, upstream, xhat, weight, weight_mine, weight_other, proj,
    out_own, out_other, branch, entry, early, active, inner_grad, sums, weight_here, proj_here, sems,
):
    core, chip, half_in, low_x = place[0], place[1], place[2], place[3]
    here, mine, others = halves(half_in, core)
    copies = fetch(
        [
            (weight.at[:, pl.ds(mult(chip * 1024, 1024), 1024)], weight_here, sems.at[0]),
            (proj.at[pl.ds(mult(low_x * 1024, 1024), 1024), :], proj_here, sems.at[1]),
        ]
    )
    bias = jnp.concatenate([vector[pl.ds(28 + low_x * 8 + n, 1), :] for n in range(8)], axis=1)
    sums[...] = jnp.zeros_like(sums)
    sums[2:3, :] = jnp.sum(upstream[0:128, :].astype(F32), axis=0, keepdims=True)
    copies[0].wait()
    for block in range(2):
        rows = pl.ds(block * 256, 256)
        inner = (
            mm(normed[rows, here], weight_here[...])
            + mm(normed[rows, mine], weight_mine[...])
            + mm(normed[rows, others], weight_other[...])
            + bias
        )
        bell = 0.5 * (1.0 + lax.erf(inner * (2.0**-0.5)))
        act = (inner * bell).astype(BF)
        active[rows, :] = act
        if block == 0:
            copies[1].wait()
        branch[rows, :] = mm(act, proj_here[...])
        slope = bell + inner * jnp.exp(-0.5 * inner * inner) * (1.0 / math.sqrt(2.0 * math.pi))
        grad = (mm(upstream[rows, :], proj_here[...], NT) * slope).astype(BF)
        inner_grad[rows, :] = grad
        sums[3:4, :] += jnp.sum(grad.astype(F32), axis=0, keepdims=True)
        for cut, part in ((here, weight_here), (mine, weight_mine), (others, weight_other)):
            back = mm(grad, part[...], NT)
            entry[rows, cut] = back * gains[2:3, cut]
            sums[0:1, cut] += jnp.sum(back * xhat[rows, cut].astype(F32), axis=0, keepdims=True)
            sums[1:2, cut] += jnp.sum(back, axis=0, keepdims=True)
    for k in range(32):
        at = (k % 8) * 128
        early[k : k + 1, :] = sums[k // 8 : k // 8 + 1, at : at + 128]

    for flip, target in ((0, out_own), (1, out_other)):
        to_core = core ^ flip
        for part in range(2):
            features = normed[:, pl.ds(mult(part * 512 + to_core * 256, 256), 256)]
            for quad in range(4):
                grads = mm(features, inner_grad[:, quad * 256 : quad * 256 + 256], TN).astype(BF)
                for n in range(2):
                    slot = part * 8 + quad * 2 + n
                    target[:, slot * 16 : slot * 16 + 16, :] = grads[:, n * 128 : n * 128 + 128].reshape(
                        16, 16, 128
                    )
        features = active[:, pl.ds(mult(to_core * 512, 512), 512)]
        for quad in range(4):
            grads = mm(features, upstream[:, quad * 256 : quad * 256 + 256], TN).astype(BF)
            for n in range(2):
                at = 256 + (quad * 2 + n) * 32
                target[:, at : at + 32, :] = grads[:, n * 128 : n * 128 + 128].reshape(16, 32, 128)


def combine_kernel(own, arrived, out):
    out[:, 0:256, :] = (own[:, 0:256, :].astype(F32) + arrived[:, 0:256, :].astype(F32)).astype(BF)
    out[:, 256:320, :] = own[:, 256:320, :]
    out[:, 320:384, :] = arrived[:, 256:320, :]


def rows_kernel(place, branch, mixed, out_weight, normed_grad, entry, gains, *outs):
    weight = out_weight[pl.ds(mult(place[3] * 256, 256), 256), :]
    for block, out in enumerate(outs):
        rows = pl.ds(block * 128, 128)
        out[0:128, :] = (branch[rows, :] + mm(mixed[rows, :], weight)).astype(BF)
        out[128:256, :] = (normed_grad[rows, :] * gains[0:1, :] + entry[rows, :]).astype(BF)


def sums_kernel(
    place, own, other, attn_gain, attn_shift, mlp_gain, mlp_shift, out_bias, qkv_bias, in_bias,
    parts, totals, columns,
):
    core, chip, half_in, low_x = place[0], place[1], place[2], place[3]
    for flip, source in ((0, own), (1, other)):
        for behind in range(4):
            part = source[:, behind * 16 : behind * 16 + 16, :].astype(F32)[:, 0:2, :]
            parts[core ^ flip, behind] = part.reshape(32, 128)
    for part in range(2):
        totals[part] = (parts[part, 0] + parts[part, 1]) + (parts[part, 2] + parts[part, 3])
    for part, first, out in (
        (1, 0, attn_gain), (1, 8, attn_shift), (0, 0, mlp_gain), (0, 8, mlp_shift), (0, 16, out_bias),
    ):
        out[...] = totals[part, pl.ds(first + half_in * 4, 4), :]
    for behind in range(4):
        origin = (chip + 4 - behind) % 4
        for k in range(3):
            columns[pl.ds(k * 8 + origin * 2, 2), :] = parts[1, behind, 16 + k * 2 : 18 + k * 2, :]
    qkv_bias[...] = columns[pl.ds(half_in * 12, 12), :]
    in_bias[pl.ds(mult(low_x * 8, 8), 8), :] = parts[0, 0, 24:32, :]
    in_bias[pl.ds(mult(8 - low_x * 8, 8), 8), :] = parts[0, 3 - low_x * 2, 24:32, :]


def finish_kernel(
    place, hidden, upstream, rows0, rows1, rows2, rows3, vector, vector_other, hidden_out, hidden_grad, bias
):
    half_in = place[2]
    bias[:, pl.ds(mult(half_in * 512, 512), 512)] = wide_row(vector, 44, 4) + wide_row(vector, 48, 4)
    bias[:, pl.ds(mult(512 - half_in * 512, 512), 512)] = wide_row(vector_other, 44, 4) + wide_row(vector_other, 48, 4)
    shares = [part.astype(F32) for part in (rows0[...], rows1[...], rows2[...], rows3[...])]
    total = (shares[0] + shares[1]) + (shares[2] + shares[3])
    full = hidden[...].astype(F32)
    hidden_out[...] = (full + total[:128] + bias[...]).astype(BF)
    xhat, scale = normalized(full)
    entry = total[128:]
    hidden_grad[...] = upstream[...].astype(F32) + scale * (
        entry
        - jnp.mean(entry, axis=1, keepdims=True)
        - xhat * jnp.mean(entry * xhat, axis=1, keepdims=True)
    )


def spread_kernel(place, piece, out, *, columns):
    for behind, slot, rows, step, at in columns:
        start = at
        if step:
            start = mult(at + ((place[1] + 4 - behind) % 4) * step, 128)
        part = piece[:, slot : slot + rows, :].astype(F32)
        out[:, pl.ds(start, 128)] = part.reshape(piece.shape[0] * rows, 128)


def spread(place, pieces, at_rows, shape_out, block, grid, in_map, out_map, columns):
    return pl.pallas_call(
        functools.partial(spread_kernel, columns=columns),
        out_shape=jax.ShapeDtypeStruct(shape_out, F32),
        grid_spec=pltpu.PrefetchScalarGridSpec(
            num_scalar_prefetch=1,
            grid=grid,
            in_specs=[pl.BlockSpec((8, at_rows, 128), in_map)],
            out_specs=pl.BlockSpec(block, out_map),
        ),
        compiler_params=pltpu.CompilerParams(vmem_limit_bytes=60 * MIB),
    )(place, pieces)


def heads_spread_kernel(place, piece, *refs):
    qkv, out = refs[-2:]
    for behind in range(4):
        start = ((place[1] + 4 - behind) % 4) * 256
        for n in range(6):
            slot = behind * 96 + n * 16
            at = mult((n // 2) * 1024 + (n % 2) * 128 + start, 128)
            qkv[:, pl.ds(at, 128)] = piece[:, slot : slot + 16, :].astype(F32).reshape(128, 128)
    for flip in range(2):
        for n in range(4):
            slot = 384 + flip * 64 + n * 16
            out[place[3] ^ flip, :, n * 128 : n * 128 + 128] = (
                piece[:, slot : slot + 16, :].astype(F32).reshape(128, 128)
            )


def heads_spread(place, pieces, flip, before=()):
    return pl.pallas_call(
        heads_spread_kernel,
        out_shape=[shape(512, 3072, dtype=F32), shape(2, 256, 1024, dtype=F32)],
        grid_spec=pltpu.PrefetchScalarGridSpec(
            num_scalar_prefetch=1,
            grid=(2,),
            in_specs=[pl.BlockSpec((8, 576, 128), lambda g, place: (g, 0, 0))]
            + [pl.BlockSpec(memory_space=pl.ANY) for _ in before],
            out_specs=[
                pl.BlockSpec((128, 3072), lambda g, place: ((place[0] ^ flip) * 2 + g, 0)),
                pl.BlockSpec((2, 128, 512), lambda g, place: (0, g, place[0] ^ flip)),
            ],
        ),
        input_output_aliases={2 + k: k for k in range(len(before))},
        compiler_params=pltpu.CompilerParams(vmem_limit_bytes=60 * MIB),
    )(place, pieces, *before)


def shape(*sizes, dtype=BF):
    return jax.ShapeDtypeStruct(sizes, dtype)


def normalized(hidden):
    moved = hidden - jnp.mean(hidden, axis=-1, keepdims=True)
    spread_out = jnp.mean(moved * moved, axis=-1, keepdims=True)
    scale = lax.rsqrt(spread_out + EPS)
    return moved * scale, scale


def per_device(
    hidden_in, doc_ids, block_map, attn_gain, attn_shift, mlp_gain, mlp_shift, qkv_weight, qkv_bias,
    out_weight, out_bias, in_weight, in_bias, proj_weight, proj_bias, cotangent,
):
    y, z = lax.axis_index("y"), lax.axis_index("z")
    xh, xl = lax.axis_index("xh"), lax.axis_index("xl")
    core = lax.axis_index("core")
    group = y * 4 + z
    chip = xh * 2 + xl
    low_half = xh == 0
    smem = whole(pltpu.SMEM)
    place = jnp.stack([core, chip, xh, xl, group]).astype(jnp.int32)

    partner = 3 - chip
    piece = jnp.concatenate(
        [
            lax.dynamic_slice(qkv_weight, (core * 256, k * 1024 + partner * 256), (256, 256))
            for k in range(3)
        ],
        axis=1,
    )
    payload = jnp.stack([hidden_in[0], cotangent[0]])
    frequency = 10000.0 ** (-(jnp.arange(0, ROT, 2).astype(F32) / ROT))
    lanes = jnp.concatenate([frequency, frequency, jnp.zeros((48,), F32)])
    lanes = jnp.concatenate([lanes, lanes])[None]
    bounds = [jnp.sum((doc_ids < label).astype(F32)).reshape(1) for label in (1, 2)]
    parts = (attn_gain, attn_shift, mlp_gain, mlp_shift, qkv_bias, in_bias, out_bias, proj_bias, *bounds)
    vector, at = jnp.zeros((7168,), F32), 0
    for part in parts:
        vector = vector + lax.pad(part.astype(F32), jnp.float32(0), [(at, 7168 - at - part.shape[0], 0)])
        at += part.shape[0]
    vector = vector.reshape(56, 128)
    piece, payload, place, lanes = lax.optimization_barrier((piece, payload, place, lanes))
    qkv_mine = cross(piece)
    qkv_other = swap(qkv_mine, "core")
    ring = [payload] + [shift_ring(payload, d) for d in (1, 2, 3)]
    in_piece = lax.dynamic_slice(in_weight, (core * 256, partner * 1024), (256, 1024))
    vector, in_piece = lax.optimization_barrier((vector, in_piece))
    vector_other = cross(vector)

    in_mine = cross(in_piece)
    in_mine, in_other = held(in_mine, swap(in_mine, "core"))

    send, normed, normed_mlp, xhat, upstream, cosine, sine, gains = call(
        project_kernel,
        [shape(16, 384, 128)]
        + [shape(512, 1024)] * 4
        + [shape(512, 128, dtype=F32)] * 2
        + [shape(4, 1024, dtype=F32)],
        [smem] * 2 + [whole()] * 7 + [whole(pl.ANY)] * 4,
        scratch=[
            pltpu.VMEM((1024, 768), BF),
            pltpu.VMEM((256, 1024), BF),
            pltpu.SemaphoreType.DMA((6,)),
        ],
    )(
        place, block_map, *ring, vector, vector_other, lanes, qkv_weight, qkv_mine, qkv_other, out_weight
    )
    heads_own = lax.all_to_all(send, PLANE, 0, 0, tiled=True)

    feed_own, feed_other, branch, entry, early = call(
        feed_kernel,
        [shape(16, 512, 128)] * 2 + [shape(512, 1024, dtype=F32)] * 2 + [shape(32, 128, dtype=F32)],
        [smem] + [whole()] * 5 + [whole(pl.ANY)] + [whole()] * 2 + [whole(pl.ANY)],
        scratch=[pltpu.VMEM((512, 1024), BF)] * 2
        + [
            pltpu.VMEM((4, 1024), F32),
            pltpu.VMEM((512, 1024), BF),
            pltpu.VMEM((1024, 1024), BF),
            pltpu.SemaphoreType.DMA((2,)),
        ],
    )(place, gains, vector, normed_mlp, upstream, xhat, in_weight, in_mine, in_other, proj_weight)
    feed_both = feed_own + swap(feed_other, "core")

    def reduce_plane(both):
        parts = lax.all_to_all(both, PLANE, 0, 0, tiled=True)
        return jnp.sum(parts.astype(F32), axis=0)

    def around(parts, rest=()):
        got = [jnp.concatenate([lax.dynamic_index_in_dim(parts, xh, 0, False), *rest])]
        for d in (1, 2, 3):
            half = ((chip + d) % 4) // 2
            got.append(
                shift_ring(jnp.concatenate([lax.dynamic_index_in_dim(parts, half, 0, False), *rest]), d)
            )
        return got

    heads_other = swap(heads_own, "core")
    heads_own, heads_other, feed_both, early, entry, branch = lax.optimization_barrier(
        (heads_own, heads_other, feed_both, early, entry, branch)
    )
    feed = reduce_plane(feed_both)
    quarter = (group % 2) * 2 + core
    bounds = jnp.where(group // 8 == xh, vector[52, :2], vector_other[52, :2])
    spot = jnp.concatenate([jnp.stack([core, quarter]).astype(jnp.int32), bounds.astype(jnp.int32)])
    back_own, back_other = call(
        attend_kernel,
        [shape(16, 320, 128)] * 2,
        [smem, smem] + [whole()] * 2,
        scratch=attend_scratch(),
        flops=45 * 10**9,
        moved=6 * MIB,
    )(spot, block_map, heads_own, heads_other)

    (returning,) = call(combine_kernel, [shape(16, 384, 128)], [whole()] * 2, limit=16)(
        back_own, swap(back_other, "core")
    )
    feed = feed.astype(BF)
    in_parts = around(feed[:256].reshape(2, 128, 128))
    proj_parts = [feed[256:], swap(feed[256:], "xl")]
    *feed_parts, returning = lax.optimization_barrier((*in_parts, *proj_parts, returning))
    feed_parts, returning = lax.optimization_barrier((jnp.concatenate(feed_parts), returning))
    feed_all = lax.all_gather(feed_parts, ("core",) + PLANE, axis=0)
    returned = lax.all_to_all(returning, PLANE, 0, 0, tiled=True)
    heads_grad_own, heads_grad_other, normed_grad, project_grad, mixed = call(
        return_kernel,
        [shape(16, 272, 128)] * 2 + [shape(512, 1024, dtype=F32), shape(512, 768), shape(512, 256)],
        [smem] + [whole()] * 6 + [whole(pl.ANY)] * 3 + [whole()],
        scratch=[
            pltpu.VMEM((2, 128, 128), BF),
            pltpu.VMEM((2, 16, 16, 128), F32),
            pltpu.VMEM((1024, 768), BF),
            pltpu.SemaphoreType.DMA((5,)),
        ],
    )(place, returned, cosine, sine, normed, xhat, upstream, qkv_weight, qkv_mine, qkv_other, early)
    heads_both = heads_grad_own + swap(heads_grad_other, "core")
    heads_sum = reduce_plane(heads_both).astype(BF)

    to_rows = call(rows_kernel, [shape(256, 1024)] * 4, [smem] + [whole()] * 6, limit=20)(
        place, branch, mixed, out_weight, normed_grad, entry, gains
    )
    heads_sum, *to_rows = lax.optimization_barrier((heads_sum, *to_rows))

    heads_parts = around(heads_sum[:192].reshape(2, 96, 128), (heads_sum[256:], heads_sum[192:256]))
    beside = jnp.where(xl == 0, heads_parts[3], heads_parts[1])
    gathering = jnp.concatenate(
        [part[:96] for part in heads_parts]
        + [heads_parts[0][112:], beside[112:]]
        + [part[96:112] for part in heads_parts]
    )
    gathering, *to_rows = lax.optimization_barrier((gathering, *to_rows))
    heads_all = to_all(gathering, PLANE, 16)

    arrived = [to_rows[0]] + [shift_ring(to_rows[d], 4 - d) for d in (1, 2, 3)]
    in_weight_grad = spread(
        place, feed_all, 512, (512, 4096), (128, 4096), (4,),
        lambda g, place: (g, 0, 0), lambda g, place: (g, 0),
        [(c, c * 128 + n * 16, 16, 1024, n * 128) for c in range(4) for n in range(8)],
    )
    proj_weight_grad = spread(
        place, feed_all, 256, (2048, 1024), (256, 1024), (2, 4),
        lambda a, g, place: (g, 2 + a, 0), lambda a, g, place: ((place[3] ^ a) * 4 + g, 0),
        [(0, n * 32, 32, 0, n * 128) for n in range(8)],
    )
    in_weight_grad, proj_weight_grad, *arrived = lax.optimization_barrier(
        (in_weight_grad, proj_weight_grad, *arrived)
    )
    hidden_out, hidden_grad = call(
        finish_kernel,
        [shape(128, 1024), shape(128, 1024, dtype=F32)],
        [smem] + [whole()] * 8,
        scratch=[pltpu.VMEM((1, 1024), F32)],
        limit=16,
    )(place, hidden_in[0], cotangent[0], *arrived, vector, vector_other)
    hidden_out, hidden_grad = hidden_out[None], hidden_grad[None]
    heads_all, in_weight_grad, proj_weight_grad, hidden_out, hidden_grad = lax.optimization_barrier(
        (heads_all, in_weight_grad, proj_weight_grad, hidden_out, hidden_grad)
    )
    heads_core = swap(heads_all, "core")

    sums = call(
        sums_kernel,
        [shape(rows, 128, dtype=F32) for rows in (4, 4, 4, 4, 4, 12, 16)],
        [smem] + [pl.BlockSpec((16, 64, 128), lambda g: (0, 8, 0))] * 2,
        scratch=[pltpu.VMEM((2, 4, 32, 128), F32), pltpu.VMEM((2, 32, 128), F32), pltpu.VMEM((24, 128), F32)],
        grid=(1,),
    )(place, heads_all, heads_core)
    (
        attn_gain_grad, attn_shift_grad, mlp_gain_grad, mlp_shift_grad, out_bias_grad, qkv_bias_grad,
        in_bias_grad,
    ) = [part.reshape(-1) for part in sums]

    partial = heads_spread(place, heads_all, 0)
    qkv_weight_grad, out_weight_grad = heads_spread(place, heads_core, 1, partial)
    out_weight_grad = out_weight_grad.reshape(512, 1024)

    return (
        hidden_out, hidden_grad, attn_gain_grad, attn_shift_grad, mlp_gain_grad, mlp_shift_grad,
        qkv_weight_grad, qkv_bias_grad, out_weight_grad, out_bias_grad, in_weight_grad, in_bias_grad,
        proj_weight_grad, out_bias_grad,
    )


def solution(mesh):
    fine = Mesh(mesh.devices.reshape(4, 4, 2, 2, 2), ("y", "z", "xl", "core", "xh"))
    ctx = ("y", "z", "xl", "core")
    rows = P("xh", ctx, None)
    half = P("xh")
    wide = P("xh", None)
    in_specs = (
        rows, wide, P(), half, half, half, half, wide, half, wide, half, wide, half, wide, half, rows,
    )
    out_specs = (
        rows, rows, half, half, half, half, wide, half, wide, half, wide, half, wide, half,
    )
    return jax.shard_map(
        per_device, mesh=fine, in_specs=in_specs, out_specs=out_specs, check_vma=False
    )
```
